256 devices in a mesh: gx: 32 (over x, y, core), gy: 8 (over z).
Axes of the slice: x: 4, y: 4, z: 8, core: 2. Of those that a mesh axis runs over, the one named last changes fastest.
Arguments:
- stencil: float32 [14, 3, 3, 64, 64, 128], P(None, None, None, 'gx', 'gy'), as said below
- candidates: float32 [8, 3, 64, 64, 128], P(None, None, 'gx', 'gy'), may hold values from -6 to 6
- segment_id: int32 [32, 32, 128], P('gx', 'gy'), may hold values from 0 to 62, as said below
Outputs:
- prolongator: float32 [8, 3, 64, 64, 128], P(None, None, 'gx', 'gy')
- coarse: float32 [8, 8, 32, 32, 63], P(None, None, 'gx', 'gy')
The draws below stay inside these ranges and needn't reach their ends.
Inputs may be any that keep to these rules, and one draw needn't show every extreme that they name: `segment_id`: in every footprint column the numbers along the third dimension start at 0 and rise by one at each new aggregate; each aggregate is a run of 2 or 4 nodes beginning at an even position, the first one of 4. `stencil`: each diagonal block is symmetric with diagonal entries at least 6 and off-diagonal entries at most 1 in magnitude.
All inputs are finite; a program needn't handle non-finite values.
Results may differ from the reference program's by a relative error of at most 0.0003.
Values sent between devices are 32-bit elements; how exact they have to be, the bound alone decides.
No kernel may reach another device: no remote copies, remote signals or barrier semaphores. Data moves between devices by JAX's collectives and lax.ppermute only.
A program may use at most 128 MiB of HBM per device.

```python
import jax
import jax.numpy as jnp
from jax import lax

NZ = 128
K = 8
ITERS = 4
NX = 64
NY = 64
FX = 32
FY = 32
NSEG = 63


def draw_stencil(key, part):
    key = jax.random.fold_in(key, 11)
    first_key, second_key, third_key = jax.random.split(key, 3)
    grid_shape = (NX, NY, NZ)
    diagonal = jax.random.uniform(first_key, (3,) + grid_shape, jnp.float32, 6.0, 10.0)
    offdiag = jax.random.uniform(second_key, (3,) + grid_shape, jnp.float32, -1.0, 1.0)
    coupling = 0.25 * jnp.clip(jax.random.normal(third_key, (13, 3, 3) + grid_shape, jnp.float32), -6.0, 6.0)
    center_block = jnp.stack([jnp.stack([diagonal[0], offdiag[0], offdiag[1]]), jnp.stack([offdiag[0], diagonal[1], offdiag[2]]), jnp.stack([offdiag[1], offdiag[2], diagonal[2]])])
    return jnp.concatenate([center_block[None], coupling], 0)


def draw_segment_id(key, part):
    key = jax.random.fold_in(key, 7)
    quads = NZ // 4
    splits = jax.random.randint(key, (FX, FY, quads), 0, 2).astype(jnp.int32)
    leading = (jnp.arange(quads) == 0)[None, None, :]
    corner = (jnp.arange(FX) == 0)[:, None, None] & (jnp.arange(FY) == 0)[None, :, None]
    splits = jnp.where(corner, 1, splits)
    splits = jnp.where(leading, 0, splits).astype(jnp.int32)
    counts = splits + 1
    starts = jnp.cumsum(counts, axis=-1).astype(jnp.int32) - counts
    cells = jnp.arange(NZ, dtype=jnp.int32)
    quad_of = cells // 4
    second_half = cells % 4 // 2
    result = starts[:, :, quad_of] + splits[:, :, quad_of] * second_half[None, None, :]
    return result.astype(jnp.int32)


def steps_of(key, dims, cuts, least, top_value):
    def one(position, blocks):
        draws = jax.random.uniform(jax.random.fold_in(jax.random.fold_in(key, 6), position), (blocks,), jnp.float32, least / len(cuts), top_value / len(cuts))
        return jnp.repeat(jnp.exp(draws), dims[position] // blocks).reshape((-1,) + (1,) * (len(dims) - position - 1))

    level = one(*cuts[0])
    for cut in cuts[1:]:
        level = level * one(*cut)
    return level


def centred(own_key, shape, scale, limit, pieces=(), kind=jnp.bfloat16):
    level = steps_of(own_key, shape, pieces, -0.22, 0.18) if pieces else 1.0
    drawn = jax.random.normal(own_key, shape, jnp.float32) * scale * level
    return jnp.minimum(jnp.maximum(drawn, -limit), limit).astype(kind)


def setup_inputs(seed: int = 0) -> dict:
    key_of = jax.random.split(jax.random.key(seed), 4)
    stencil = draw_stencil(jax.random.fold_in(key_of[3], 71), 0)
    candidates = centred(key_of[1], (K, 3, NX, NY, NZ), 1.0, 6.0, ((2, 32), (3, 8)), jnp.float32)
    segment_id = draw_segment_id(jax.random.fold_in(key_of[3], 71), 0)
    return dict(stencil=stencil, candidates=candidates, segment_id=segment_id)


damping = 0.8
neighbour_steps = [(sx, sy, sz) for sx in (-1, 0, 1) for sy in (-1, 0, 1) for sz in (-1, 0, 1) if (sx, sy, sz) > (0, 0, 0)]
cyclic_up = (1, 2, 0)
cyclic_down = (2, 0, 1)

def block_apply(matrix, vectors, flipped):
    outputs = []
    for row_index in range(3):
        if flipped:
            entries = [matrix[column, row_index] for column in range(3)]
        else:
            entries = [matrix[row_index, column] for column in range(3)]
        summed = entries[0][None] * vectors[:, 0] + entries[1][None] * vectors[:, 1] + entries[2][None] * vectors[:, 2]
        outputs.append(summed)
    return jnp.stack(outputs, 1)

def invert(blocks):
    cofactor = []
    for row_index in range(3):
        line = []
        for column in range(3):
            up_row, down_row = (cyclic_up[row_index], cyclic_down[row_index])
            up_col, down_col = (cyclic_up[column], cyclic_down[column])
            line.append(blocks[up_row, up_col] * blocks[down_row, down_col] - blocks[up_row, down_col] * blocks[down_row, up_col])
        cofactor.append(line)
    determinant = blocks[0, 0] * cofactor[0][0] + blocks[0, 1] * cofactor[0][1] + blocks[0, 2] * cofactor[0][2]
    return jnp.stack([jnp.stack([cofactor[column][row_index] / determinant for column in range(3)]) for row_index in range(3)])

def operate(field_pad, coupling):
    size_x, size_y, size_z = (field_pad.shape[2], field_pad.shape[3], field_pad.shape[4])
    field_z = jnp.pad(field_pad, ((0, 0), (0, 0), (0, 0), (0, 0), (1, 1)))
    coupling_z = jnp.pad(coupling, ((0, 0), (0, 0), (0, 0), (0, 0), (0, 0), (1, 1)))

    def window(array, step_x, step_y, step_z):
        return array[..., 1 + step_x:size_x - 1 + step_x, 1 + step_y:size_y - 1 + step_y, 1 + step_z:size_z + 1 + step_z]
    result = block_apply(window(coupling_z[0], 0, 0, 0), window(field_z, 0, 0, 0), False)
    for index, (step_x, step_y, step_z) in enumerate(neighbour_steps):
        result = result + block_apply(window(coupling_z[1 + index], 0, 0, 0), window(field_z, step_x, step_y, step_z), False)
        result = result + block_apply(window(coupling_z[1 + index], -step_x, -step_y, -step_z), window(field_z, -step_x, -step_y, -step_z), True)
    return result

def sweep(field_pad, coupling, inverse):
    residual_field = operate(field_pad, coupling)
    inner = field_pad[:, :, 1:-1, 1:-1]
    return inner - damping * block_apply(inverse, residual_field, False)

def factor(row_data, segments):
    cands = row_data.shape[0]
    count_x, count_y, depth = segments.shape
    indicator = (segments[..., None] == jnp.arange(NSEG, dtype=jnp.int32)).astype(jnp.float32)
    blocks = row_data.reshape(cands, 3, count_x, 2, count_y, 2, depth)

    def column_sum(values):
        partial_value = values.sum(axis=(0, 2, 4))
        return jnp.einsum('abz,abzs->abs', partial_value, indicator, precision=lax.Precision.HIGHEST)

    def spread(values):
        return jnp.einsum('abs,abzs->abz', values, indicator, precision=lax.Precision.HIGHEST)[None, :, None, :, None, :]
    columns = [blocks[index] for index in range(cands)]
    factors = [[None] * cands for index in range(cands)]
    for first in range(cands):
        length = jnp.sqrt(column_sum(columns[first] * columns[first]))
        columns[first] = columns[first] / spread(length)
        factors[first][first] = length
        for second in range(first + 1, cands):
            inner_prod = column_sum(columns[first] * columns[second])
            factors[first][second] = inner_prod
            columns[second] = columns[second] - spread(inner_prod) * columns[first]
    zeros = jnp.zeros_like(factors[0][0])
    upper = jnp.stack([jnp.stack([factors[first][second] if second >= first else zeros for second in range(cands)]) for first in range(cands)])
    return (jnp.stack(columns).reshape(row_data.shape), upper)

def wrap_rim(array):
    widths = [(0, 0)] * (array.ndim - 3) + [(1, 1), (1, 1), (0, 0)]
    return jnp.pad(array, widths, mode='wrap')

def reference(stencil, candidates, segment_id):
    inverse = invert(stencil[0])
    coupling = wrap_rim(stencil)
    smoothed = candidates
    for sweep_index in range(ITERS):
        smoothed = sweep(wrap_rim(smoothed), coupling, inverse)
    rolled = jnp.roll(smoothed, (-1, -1), axis=(2, 3))
    columns, upper = factor(rolled, segment_id)
    return (jnp.roll(columns, (1, 1), axis=(2, 3)), upper)
```

```python
import functools

import jax
import jax.numpy as jnp
import numpy as np
from jax import lax
from jax.experimental import pallas as pl
from jax.experimental.pallas import tpu as pltpu
from jax.sharding import PartitionSpec as P

ITERS = 4
NSEG = 63
K = 8
DAMPING = 0.8
F32 = jnp.float32
neighbour_steps = [
    (sx, sy, sz)
    for sx in (-1, 0, 1)
    for sy in (-1, 0, 1)
    for sz in (-1, 0, 1)
    if (sx, sy, sz) > (0, 0, 0)
]
ROLLED = [j for j, o in enumerate(neighbour_steps) if o[2] != 0]
SYM = [(0, 0), (0, 1), (0, 2), (1, 1), (1, 2), (2, 2)]
SYM_OF = {(e, d): SYM.index((min(e, d), max(e, d))) for e in range(3) for d in range(3)}
ROWS = 24
VMEM = pl.BlockSpec(memory_space=pltpu.VMEM)
ANY = pl.BlockSpec(memory_space=pl.ANY)
LIMIT = 12 * 2**20

N_V4 = 48
N_S4 = 2 * (6 + 117)
V4, S4 = 0, 4 * N_V4
V1 = 4 * (N_V4 + N_S4)
S1 = V1 + 48
ONE_DN = [j for j, o in enumerate(neighbour_steps) if o[1] == -1]
ONE_UP = [j for j, o in enumerate(neighbour_steps) if o[1] == 1]
SEG_ROW = S1 + 18 * len(ONE_UP)
MSG_DN = -(-(S1 + 18 * len(ONE_DN)) // 8) * 8
MSG_UP = -(-(SEG_ROW + 1) // 8) * 8


def call(kernel, out_shape, *args, flops=0, aliases=None):
    return pl.pallas_call(
        kernel,
        out_shape=out_shape,
        in_specs=[VMEM] * len(args),
        out_specs=jax.tree.map(lambda _: VMEM, out_shape),
        input_output_aliases=aliases or {},
        compiler_params=pltpu.CompilerParams(vmem_limit_bytes=LIMIT),
        cost_estimate=pl.CostEstimate(flops=flops, bytes_accessed=0, transcendentals=0),
    )(*args)


def struct(*shape):
    return jax.ShapeDtypeStruct(shape, F32)


def invert(b):
    a00, a01, a02, a11, a12, a22 = b
    c00 = a11 * a22 - a12 * a12
    c01 = a12 * a02 - a01 * a22
    c02 = a01 * a12 - a11 * a02
    c11 = a00 * a22 - a02 * a02
    c12 = a01 * a02 - a00 * a12
    c22 = a00 * a11 - a01 * a01
    det = a00 * c00 + a01 * c01 + a02 * c02
    return [c / det for c in (c00, c01, c02, c11, c12, c22)]


def pack_kernel(stencil, cands, seg, dn, up, inv):
    for p in range(2):
        blocks = [stencil[0, e, d, p] for e, d in SYM]
        for i, entry in enumerate(invert(blocks)):
            inv[i, p] = entry
    for c in range(K):
        for d in range(3):
            for p in range(2):
                i = (c * 3 + d) * 2 + p
                dn[pl.ds(V4 + 4 * i, 4), :] = cands[c, d, p, 0:4]
                up[pl.ds(V4 + 4 * i, 4), :] = cands[c, d, p, 4:8]
                dn[pl.ds(V1 + i, 1), :] = cands[c, d, p, 4:5]
                up[pl.ds(V1 + i, 1), :] = cands[c, d, p, 3:4]
    for i in range(6):
        for p in range(2):
            k = i * 2 + p
            dn[pl.ds(S4 + 4 * k, 4), :] = inv[i, p, 0:4]
            up[pl.ds(S4 + 4 * k, 4), :] = inv[i, p, 4:8]
    for j in range(13):
        for e in range(3):
            for d in range(3):
                for p in range(2):
                    k = 12 + ((j * 3 + e) * 3 + d) * 2 + p
                    dn[pl.ds(S4 + 4 * k, 4), :] = stencil[1 + j, e, d, p, 0:4]
                    up[pl.ds(S4 + 4 * k, 4), :] = stencil[1 + j, e, d, p, 4:8]
    for msg, ones, row in ((dn, ONE_DN, 4), (up, ONE_UP, 3)):
        for n, j in enumerate(ones):
            for e in range(3):
                for d in range(3):
                    for p in range(2):
                        at = S1 + n * 18 + (e * 3 + d) * 2 + p
                        msg[pl.ds(at, 1), :] = stencil[1 + j, e, d, p, row : row + 1]
    up[pl.ds(SEG_ROW, 1), :] = seg[0, 3:4].astype(F32)


def roll_z(x, by):
    return pltpu.roll(x, by % 128, x.ndim - 1)


def own_kernel(stencil, cands, inv, coef, rolled, inverse, field):
    own = pl.ds(8, 8)
    for c in range(K):
        for d in range(3):
            field[c * 3 + d, :, own, :] = cands[c, d]
    for i in range(6):
        inverse[i, :, own, :] = inv[i]
    for j in range(13):
        for e in range(3):
            for d in range(3):
                block = stencil[1 + j, e, d]
                coef[j * 9 + e * 3 + d, :, own, :] = block
                if j in ROLLED:
                    rolled[ROLLED.index(j) * 9 + e * 3 + d, :, own, :] = roll_z(
                        block, neighbour_steps[j][2]
                    )


def halo_kernel(from_up, from_dn, coef_in, rolled_in, inverse_in, field_in, coef, rolled, inverse, field):
    for msg, four, one, ones in ((from_up, 16, 20, ONE_DN), (from_dn, 4, 3, ONE_UP)):
        for i in range(24):
            for p in range(2):
                field[i, p, pl.ds(four, 4), :] = msg[pl.ds(V4 + 4 * (2 * i + p), 4), :]
                field[i, p, pl.ds(one, 1), :] = msg[pl.ds(V1 + 2 * i + p, 1), :]
        for i in range(6):
            for p in range(2):
                inverse[i, p, pl.ds(four, 4), :] = msg[pl.ds(S4 + 4 * (2 * i + p), 4), :]
        for j in range(13):
            for n in range(9):
                k = 12 + (j * 9 + n) * 2
                pair = msg[pl.ds(S4 + 4 * k, 8), :]
                coef[j * 9 + n, 0, pl.ds(four, 4), :] = pair[0:4]
                coef[j * 9 + n, 1, pl.ds(four, 4), :] = pair[4:8]
                if j in ROLLED:
                    pair = roll_z(pair, neighbour_steps[j][2])
                    rolled[ROLLED.index(j) * 9 + n, 0, pl.ds(four, 4), :] = pair[0:4]
                    rolled[ROLLED.index(j) * 9 + n, 1, pl.ds(four, 4), :] = pair[4:8]
        for m, j in enumerate(ones):
            for n in range(9):
                for p in range(2):
                    at = S1 + m * 18 + n * 2 + p
                    coef[j * 9 + n, p, pl.ds(one, 1), :] = msg[pl.ds(at, 1), :]


def gather_terms(coef, rolled, field, base, half, terms):
    lane = lax.broadcasted_iota(jnp.int32, (8, 128), 1)
    acc = {}
    loads = {}

    def value(c, d, plane, oy):
        key = (c, d, plane, oy)
        if key not in loads:
            loads[key] = field[(half * 4 + c) * 3 + d, plane, pl.ds(base + oy, 8), :]
        return loads[key]

    for cp, fp, j, transposed in sorted(terms, key=lambda t: (t[1], -neighbour_steps[t[2]][1] if t[3] else neighbour_steps[t[2]][1])):
        ox, oy, oz = neighbour_steps[j]
        for d in range(3):
            for e in range(3):
                if transposed:
                    m = coef[j * 9 + d * 3 + e, cp, pl.ds(base - oy, 8), :]
                    shift, row = -oz, -oy
                elif oz:
                    m = rolled[ROLLED.index(j) * 9 + e * 3 + d, cp, pl.ds(base, 8), :]
                    shift, row = oz, oy
                else:
                    m = coef[j * 9 + e * 3 + d, cp, pl.ds(base, 8), :]
                    shift, row = 0, oy
                for c in range(4):
                    t = m * value(c, d, fp, row)
                    key = (c, e, shift)
                    acc[key] = acc[key] + t if key in acc else t
    out = []
    for c in range(4):
        line = []
        for e in range(3):
            total = acc[c, e, 0]
            total = total + jnp.where(lane < 127, roll_z(acc[c, e, 1], -1), 0.0)
            total = total + jnp.where(lane > 0, roll_z(acc[c, e, -1], 1), 0.0)
            line.append(total)
        out.append(line)
    return out


FLAT = [j for j, o in enumerate(neighbour_steps) if o[0] == 0]
STEP = [j for j, o in enumerate(neighbour_steps) if o[0] == 1]
TERMS = [
    [(0, 0, j, t) for j in FLAT for t in (False, True)] + [(0, 1, j, False) for j in STEP],
    [(1, 1, j, t) for j in FLAT for t in (False, True)] + [(0, 0, j, True) for j in STEP],
]
OUT_TERMS = [(1, 1, j, True) for j in STEP]
IN_TERMS = [(1, 0, j, False) for j in STEP]


def outgoing(coef, field, push):
    def step(i, carry):
        tile, half = i // 2, i % 2
        base = 4 + 8 * tile
        got = gather_terms(coef, None, field, base, half, OUT_TERMS)
        for c in range(4):
            for e in range(3):
                push[(half * 4 + c) * 3 + e, pl.ds(pl.multiple_of(8 * tile, 8), 8), :] = got[c][e]
        return carry

    lax.fori_loop(0, 4, step, 0)


def plane_out(field, pull):
    for i in range(24):
        pull[i] = field[i, 0]


def first_kernel(coef, field, push, pull):
    plane_out(field, pull)
    outgoing(coef, field, push)


def local_kernel(coef, rolled, field, part):
    def step(i, carry):
        tile, half = i // 2, i % 2
        base = 4 + 8 * tile
        for p in range(2):
            got = gather_terms(coef, rolled, field, base, half, TERMS[p])
            for c in range(4):
                for e in range(3):
                    part[(half * 4 + c) * 3 + e, p, pl.ds(pl.multiple_of(8 * tile, 8), 8), :] = got[c][e]
        return carry

    lax.fori_loop(0, 4, step, 0)


def finish(coef, rolled, inverse, field, part, pushed, pulled, new):
    def step(i, carry):
        tile, half = i // 2, i % 2
        base = 4 + 8 * tile
        rows = pl.ds(pl.multiple_of(8 * tile, 8), 8)
        got = gather_terms(coef, rolled, pulled, base, half, IN_TERMS)
        for p in range(2):
            inv = [inverse[n, p, pl.ds(base, 8), :] * DAMPING for n in range(6)]
            for c in range(4):
                at = (half * 4 + c) * 3
                res = [
                    part[at + e, p, rows, :] + (got[c][e] if p else pushed[at + e, rows, :])
                    for e in range(3)
                ]
                for e in range(3):
                    v = field[at + e, p, pl.ds(base, 8), :]
                    step_ = (
                        inv[SYM_OF[e, 0]] * res[0]
                        + inv[SYM_OF[e, 1]] * res[1]
                        + inv[SYM_OF[e, 2]] * res[2]
                    )
                    new[at + e, p, pl.ds(base, 8), :] = (1.0 - DAMPING) * v - step_
        return carry

    lax.fori_loop(0, 4, step, 0)


def sweep_kernel(coef, rolled, inverse, field, part, pushed, pulled, new, push, pull):
    finish(coef, rolled, inverse, field, part, pushed, pulled, new)
    plane_out(new, pull)
    outgoing(coef, new, push)


def last_kernel(coef, rolled, inverse, field, part, pushed, pulled, new, to_dn, to_up):
    finish(coef, rolled, inverse, field, part, pushed, pulled, new)
    for i in range(24):
        to_dn[i] = new[i, 0]
        to_up[i] = new[i, 1]


def segments_kernel(seg, from_dn, frame):
    frame[0] = jnp.zeros((8, 128), F32)
    frame[0, pl.ds(0, 1), :] = from_dn[pl.ds(SEG_ROW, 1), :]
    frame[0, pl.ds(1, 4), :] = seg[0].astype(F32)


def qr_kernel(field, lower, upper_plane, seg, seg_lower, prolongator, coarse, q):
    lane = lax.broadcasted_iota(jnp.int32, (8, 128), 1)
    even = lane % 2 == 0
    valid_row = lax.broadcasted_iota(jnp.int32, (8, 128), 0) < 5

    def planes(fx):
        if fx == 0:
            return [lambda i, s: lower[i, s, :], lambda i, s: field[i, 0, s, :]]
        return [lambda i, s: field[i, 1, s, :], lambda i, s: upper_plane[i, s, :]]

    starts = None
    for fx in range(2):
        ids = (seg_lower if fx == 0 else seg)[0]
        joins_next = (ids == roll_z(ids, -2)) & (lane < 126)
        joins_prev = (ids == roll_z(ids, 2)) & (lane >= 2)

        def total(x):
            x = x + jnp.where(even, roll_z(x, -1), roll_z(x, 1))
            return x + jnp.where(joins_next, roll_z(x, -2), 0.0) + jnp.where(joins_prev, roll_z(x, 2), 0.0)

        def dot(a, b):
            s = a[0] * b[0]
            t = a[1] * b[1]
            u = a[2] * b[2]
            for n in range(3, 12, 3):
                s = s + a[n] * b[n]
                t = t + a[n + 1] * b[n + 1]
                u = u + a[n + 2] * b[n + 2]
            return total(s + t + u)

        if fx == 1:
            slot = lane.astype(F32)
            found = jnp.zeros((8, 128), jnp.int32)
            for bit in (64, 32, 16, 8, 4, 2, 1):
                before = jnp.take_along_axis(ids, found + (bit - 1), axis=1)
                found = jnp.where(before < slot, found + bit, found)
            top = jnp.max(ids, axis=1, keepdims=True)
            starts = found
            in_use = slot <= top

            def put(k, j, values):
                compact = jnp.take_along_axis(values, starts, axis=1)
                compact = jnp.where(in_use, compact, 0.0)
                coarse[k, j, 0] = compact[1:5, 0:NSEG]

        cols = []
        for i in range(K):
            col = []
            for get in planes(fx):
                for first in (7, 8):
                    for d in range(3):
                        col.append(get(i * 3 + d, pl.ds(first, 8, stride=2)))
            cols.append([jnp.where(valid_row, x, 1.0) for x in col])
        for k in range(K):
            length = jnp.sqrt(dot(cols[k], cols[k]))
            scale = 1.0 / length
            cols[k] = [x * scale for x in cols[k]]
            if fx == 1:
                put(k, k, length)
            for j in range(k + 1, K):
                r = dot(cols[k], cols[j])
                cols[j] = [x - r * y for x, y in zip(cols[j], cols[k])]
                if fx == 1:
                    put(k, j, r)
                    coarse[j, k, 0] = jnp.zeros((4, NSEG), F32)
            member = 1 - fx
            for d in range(3):
                odd_first = cols[k][member * 6 + d]
                even_first = cols[k][member * 6 + 3 + d]
                prolongator[k, d, fx, pl.ds(0, 4, stride=2), :] = even_first[0:4]
                prolongator[k, d, fx, pl.ds(1, 4, stride=2), :] = odd_first[1:5]


def moved(block, axis, by):
    size = lax.axis_size(axis)
    return lax.ppermute(block, axis, [((i + by) % size, i) for i in range(size)])


def body(stencil, cands, seg):
    msg_dn, msg_up, inv = call(
        pack_kernel,
        [struct(MSG_DN, 128), struct(MSG_UP, 128), struct(6, 2, 8, 128)],
        stencil, cands, seg,
    )
    from_up = moved(msg_dn, "gy", 1)
    from_dn = moved(msg_up, "gy", -1)
    frames = [struct(117, 2, ROWS, 128), struct(9 * len(ROLLED), 2, ROWS, 128), struct(6, 2, ROWS, 128), struct(24, 2, ROWS, 128)]
    own = call(own_kernel, frames, stencil, cands, inv, flops=10**7)
    coef, rolled, inverse, field = call(
        halo_kernel, frames, from_up, from_dn, *own, aliases={2: 0, 3: 1, 4: 2, 5: 3}
    )
    segs = call(segments_kernel, [struct(1, 8, 128)], seg, from_dn)[0]
    side = [struct(24, 16, 128), struct(24, ROWS, 128)]
    push, pull = call(first_kernel, side, coef, field)
    seg_lower = moved(segs, "gx", -1)
    for t in range(ITERS):
        pushed = moved(push, "gx", -1)
        pulled = moved(pull, "gx", 1)
        part = call(local_kernel, [struct(24, 2, 16, 128)], coef, rolled, field, flops=10**7)[0]
        pulled = pulled.reshape(24, 1, ROWS, 128)
        args = (coef, rolled, inverse, field, part, pushed, pulled)
        if t < ITERS - 1:
            field, push, pull = call(sweep_kernel, [frames[3]] + side, *args)
        else:
            field, to_dn, to_up = call(last_kernel, [frames[3]] + [struct(24, ROWS, 128)] * 2, *args)
    lower = moved(to_up, "gx", -1)
    upper_plane = moved(to_dn, "gx", 1)
    prolongator, coarse = pl.pallas_call(
        qr_kernel,
        out_shape=[struct(K, 3, 2, 8, 128), struct(K, K, 1, 4, NSEG)],
        in_specs=[VMEM] * 5,
        out_specs=[VMEM] * 2,
        scratch_shapes=[pltpu.VMEM((8, 12, 8, 128), F32)],
        compiler_params=pltpu.CompilerParams(vmem_limit_bytes=LIMIT),
    )(field, lower, upper_plane, segs, seg_lower)
    return prolongator, coarse


def solution(mesh):
    in_specs = (
        P(None, None, None, "gx", "gy", None),
        P(None, None, "gx", "gy", None),
        P("gx", "gy", None),
    )
    out_specs = (P(None, None, "gx", "gy", None), P(None, None, "gx", "gy", None))
    return jax.shard_map(body, mesh=mesh, in_specs=in_specs, out_specs=out_specs, check_vma=False)
```

```python
import functools

import jax
import jax.numpy as jnp
import numpy as np
from jax import lax
from jax.experimental import pallas as pl
from jax.experimental.pallas import tpu as pltpu
from jax.sharding import PartitionSpec as P

ITERS = 4
NSEG = 63
K = 8
DAMPING = 0.8
F32 = jnp.float32
neighbour_steps = [
    (sx, sy, sz)
    for sx in (-1, 0, 1)
    for sy in (-1, 0, 1)
    for sz in (-1, 0, 1)
    if (sx, sy, sz) > (0, 0, 0)
]
ROLLED = [j for j, o in enumerate(neighbour_steps) if o[2] != 0]
SYM = [(0, 0), (0, 1), (0, 2), (1, 1), (1, 2), (2, 2)]
SYM_OF = {(e, d): SYM.index((min(e, d), max(e, d))) for e in range(3) for d in range(3)}
ROWS = 24
VMEM = pl.BlockSpec(memory_space=pltpu.VMEM)
LIMIT = 12 * 2**20

ONE_DN = [j for j, o in enumerate(neighbour_steps) if o[1] == -1]
ONE_UP = [j for j, o in enumerate(neighbour_steps) if o[1] == 1]
RIM_S = 48
RIM = 160
HALO = 4 * 2 * (6 + 117)
SEG_ROW = 4 * 48
EDGE = SEG_ROW + 8
PAD = 8


def call(kernel, out_shape, *args, flops=0, aliases=None, scratch=()):
    return pl.pallas_call(
        kernel,
        out_shape=out_shape,
        in_specs=[VMEM] * (len(args)),
        out_specs=jax.tree.map(lambda _: VMEM, out_shape),
        input_output_aliases=aliases or {},
        scratch_shapes=list(scratch),
        compiler_params=pltpu.CompilerParams(vmem_limit_bytes=LIMIT),
        cost_estimate=pl.CostEstimate(flops=flops, bytes_accessed=0, transcendentals=0),
    )(*args)


def parity():
    return lax.rem(lax.axis_index("gx"), 2)


def struct(*shape):
    return jax.ShapeDtypeStruct(shape, F32)


def invert(b):
    a00, a01, a02, a11, a12, a22 = b
    c00 = a11 * a22 - a12 * a12
    c01 = a12 * a02 - a01 * a22
    c02 = a01 * a12 - a11 * a02
    c11 = a00 * a22 - a02 * a02
    c12 = a01 * a02 - a00 * a12
    c22 = a00 * a11 - a01 * a01
    det = a00 * c00 + a01 * c01 + a02 * c02
    return [c / det for c in (c00, c01, c02, c11, c12, c22)]


def pack_kernel(stencil, cands, rim_dn, rim_up, coef, rolled, inverse, field):
    own = pl.ds(8, 8)
    for c in range(K):
        for d in range(3):
            field[c * 3 + d, :, own, :] = cands[c, d]
    for p in range(2):
        blocks = [stencil[0, e, d, p] for e, d in SYM]
        for i, entry in enumerate(invert(blocks)):
            inverse[i, p, own, :] = entry
    for j in range(13):
        for e in range(3):
            for d in range(3):
                block = stencil[1 + j, e, d]
                coef[j * 9 + e * 3 + d, :, own, :] = block
                if j in ROLLED:
                    rolled[ROLLED.index(j) * 9 + e * 3 + d, :, own, :] = roll_z(
                        block, neighbour_steps[j][2]
                    )
    for c in range(K):
        for d in range(3):
            for p in range(2):
                i = (c * 3 + d) * 2 + p
                rim_dn[pl.ds(i, 1), :] = cands[c, d, p, 0:1]
                rim_up[pl.ds(i, 1), :] = cands[c, d, p, 7:8]
    for msg, ones, row in ((rim_dn, ONE_DN, 0), (rim_up, ONE_UP, 7)):
        for n, j in enumerate(ones):
            for e in range(3):
                for d in range(3):
                    for p in range(2):
                        at = RIM_S + n * 18 + (e * 3 + d) * 2 + p
                        msg[pl.ds(at, 1), :] = stencil[1 + j, e, d, p, row : row + 1]


def roll_z(x, by):
    return pltpu.roll(x, by % 128, x.ndim - 1)


def pack_halo_kernel(stencil, inverse, halo_dn, halo_up):
    for i in range(6):
        for p in range(2):
            k = i * 2 + p
            halo_dn[pl.ds(4 * k, 4), :] = inverse[i, p, pl.ds(8, 4), :]
            halo_up[pl.ds(4 * k, 4), :] = inverse[i, p, pl.ds(12, 4), :]
    for j in range(13):
        for e in range(3):
            for d in range(3):
                for p in range(2):
                    k = 12 + ((j * 3 + e) * 3 + d) * 2 + p
                    halo_dn[pl.ds(4 * k, 4), :] = stencil[1 + j, e, d, p, 0:4]
                    halo_up[pl.ds(4 * k, 4), :] = stencil[1 + j, e, d, p, 4:8]


def halo_kernel(from_up, from_dn, coef_in, rolled_in, inverse_in, coef, rolled, inverse):
    for msg, four in ((from_up, 16), (from_dn, 4)):
        for i in range(6):
            for p in range(2):
                inverse[i, p, pl.ds(four, 4), :] = msg[pl.ds(4 * (2 * i + p), 4), :]
        for j in range(13):
            for n in range(9):
                k = 12 + (j * 9 + n) * 2
                pair = msg[pl.ds(4 * k, 8), :]
                coef[j * 9 + n, 0, pl.ds(four, 4), :] = pair[0:4]
                coef[j * 9 + n, 1, pl.ds(four, 4), :] = pair[4:8]
                if j in ROLLED:
                    pair = roll_z(pair, neighbour_steps[j][2])
                    rolled[ROLLED.index(j) * 9 + n, 0, pl.ds(four, 4), :] = pair[0:4]
                    rolled[ROLLED.index(j) * 9 + n, 1, pl.ds(four, 4), :] = pair[4:8]


def gather_terms(coef, rolled, load, base, half, terms):
    lane = lax.broadcasted_iota(jnp.int32, (8, 128), 1)
    acc = {}
    loads = {}

    def value(c, d, plane, oy):
        key = (c, d, plane, oy)
        if key not in loads:
            loads[key] = load((half * 4 + c) * 3 + d, plane, base + oy)
        return loads[key]

    for cp, fp, j, transposed in sorted(terms, key=lambda t: (t[1], -neighbour_steps[t[2]][1] if t[3] else neighbour_steps[t[2]][1])):
        ox, oy, oz = neighbour_steps[j]
        for d in range(3):
            for e in range(3):
                if transposed:
                    m = coef[j * 9 + d * 3 + e, cp, pl.ds(base - oy, 8), :]
                    shift, row = -oz, -oy
                elif oz:
                    m = rolled[ROLLED.index(j) * 9 + e * 3 + d, cp, pl.ds(base, 8), :]
                    shift, row = oz, oy
                else:
                    m = coef[j * 9 + e * 3 + d, cp, pl.ds(base, 8), :]
                    shift, row = 0, oy
                for c in range(4):
                    t = m * value(c, d, fp, row)
                    key = (c, e, shift)
                    acc[key] = acc[key] + t if key in acc else t
    out = []
    for c in range(4):
        line = []
        for e in range(3):
            total = acc[c, e, 0]
            total = total + jnp.where(lane < 127, roll_z(acc[c, e, 1], -1), 0.0)
            total = total + jnp.where(lane > 0, roll_z(acc[c, e, -1], 1), 0.0)
            line.append(total)
        out.append(line)
    return out


FLAT = [j for j, o in enumerate(neighbour_steps) if o[0] == 0]
STEP = [j for j, o in enumerate(neighbour_steps) if o[0] == 1]
TERMS = [
    [(0, 0, j, t) for j in FLAT for t in (False, True)] + [(0, 1, j, False) for j in STEP],
    [(1, 1, j, t) for j in FLAT for t in (False, True)] + [(0, 0, j, True) for j in STEP],
]
OUT_TERMS = [(1, 1, j, True) for j in STEP]
IN_TERMS = [(1, 0, j, False) for j in STEP]


def from_frame(field):
    return lambda i, plane, row: field[i, plane, pl.ds(row, 8), :]


def tiles(bases, step):
    if len(bases) == 1:
        for half in range(2):
            step(bases[0], half)
        return

    def one(i, carry):
        step(bases[0] + (i // 2) * 8, i % 2)
        return carry

    lax.fori_loop(0, 2 * len(bases), one, 0)


def side_rows(lo, hi, items):
    return PAD + items * (hi - lo) + PAD


def spot(i, row, lo, hi):
    return PAD + i * (hi - lo) + row - lo


def outgoing(coef, field, msg, slot, bases, lo, hi):
    def step(base, half):
        got = gather_terms(coef, None, from_frame(field), base, half, OUT_TERMS)
        for c in range(4):
            for e in range(3):
                i = (half * 4 + c) * 3 + e
                msg[slot, pl.ds(spot(i, base, lo, hi), 8), :] = got[c][e]

    tiles(bases, step)


def plane_out(field, plane, msg, slot, lo, hi):
    for i in range(24):
        msg[slot, pl.ds(spot(i, lo, lo, hi), hi - lo), :] = field[i, plane, pl.ds(lo, hi - lo), :]


def send(coef, field, box, same, other, bases, lo, hi):
    right = parity()
    outgoing(coef, field, box, right, bases, lo, hi)
    plane_out(field, 0, box, 1 - right, lo, hi)
    same[...] = box[0]
    other[...] = box[1]


def first_kernel(from_up, from_dn, coef_in, field_in, coef, field, same, other, box):
    for msg, row, ones in ((from_up, 16, ONE_DN), (from_dn, 7, ONE_UP)):
        for i in range(24):
            for p in range(2):
                field[i, p, pl.ds(row, 1), :] = msg[pl.ds(2 * i + p, 1), :]
        for m, j in enumerate(ones):
            for n in range(9):
                for p in range(2):
                    at = RIM_S + m * 18 + n * 2 + p
                    coef[j * 9 + n, p, pl.ds(row, 1), :] = msg[pl.ds(at, 1), :]
    send(coef, field, box, same, other, *ROUNDS[0])


def second_kernel(from_up, from_dn, coef, field_in, field, same, other, box):
    for msg, row in ((from_up, 16), (from_dn, 4)):
        for i in range(24):
            for p in range(2):
                field[i, p, pl.ds(row, 4), :] = msg[pl.ds(4 * (2 * i + p), 4), :]
    send(coef, field, box, same, other, *ROUNDS[1])


def local_kernel(bases, coef, rolled, field, part):
    def step(base, half):
        for p in range(2):
            got = gather_terms(coef, rolled, from_frame(field), base, half, TERMS[p])
            for c in range(4):
                for e in range(3):
                    part[(half * 4 + c) * 3 + e, p, pl.ds(base, 8), :] = got[c][e]

    tiles(bases, step)


def finish(coef, rolled, inverse, field, part, same, other, box, new, bases, lo, hi):
    box[0] = same[...]
    box[1] = other[...]
    right = parity()

    def load(i, plane, row):
        return box[right, pl.ds(spot(i, row, lo, hi), 8), :]

    def step(base, half):
        got = gather_terms(coef, rolled, load, base, half, IN_TERMS)
        for p in range(2):
            inv = [inverse[n, p, pl.ds(base, 8), :] * DAMPING for n in range(6)]
            for c in range(4):
                at = (half * 4 + c) * 3
                res = []
                for e in range(3):
                    far = got[c][e] if p else box[1 - right, pl.ds(spot(at + e, base, lo, hi), 8), :]
                    res.append(part[at + e, p, pl.ds(base, 8), :] + far)
                for e in range(3):
                    v = field[at + e, p, pl.ds(base, 8), :]
                    move = (
                        inv[SYM_OF[e, 0]] * res[0]
                        + inv[SYM_OF[e, 1]] * res[1]
                        + inv[SYM_OF[e, 2]] * res[2]
                    )
                    new[at + e, p, pl.ds(base, 8), :] = (1.0 - DAMPING) * v - move

    tiles(bases, step)


ROUNDS = [((8,), 7, 17), ((4, 12), 4, 20), ((4, 12), 5, 19), ((4, 12), 5, 19)]
QR_LO, QR_HI = 7, 17


def sweep_first(coef, rolled, inverse, field, part, same, other, seg, new, to_dn, to_up, box):
    finish(coef, rolled, inverse, field, part, same, other, box, new, *ROUNDS[0])
    for i in range(24):
        for p in range(2):
            to_dn[pl.ds(4 * (2 * i + p), 4), :] = new[i, p, pl.ds(8, 4), :]
            to_up[pl.ds(4 * (2 * i + p), 4), :] = new[i, p, pl.ds(12, 4), :]
    to_up[pl.ds(SEG_ROW, 1), :] = seg[0, 3:4].astype(F32)


def sweep_kernel(t, coef, rolled, inverse, field, part, same, other, new, same_out, other_out, box, box_out):
    finish(coef, rolled, inverse, field, part, same, other, box, new, *ROUNDS[t])
    send(coef, new, box_out, same_out, other_out, *ROUNDS[t + 1])


def last_kernel(coef, rolled, inverse, field, part, same, other, segs, new, same_out, other_out, box, box_out):
    finish(coef, rolled, inverse, field, part, same, other, box, new, *ROUNDS[-1])
    right = parity()
    plane_out(new, 1, box_out, right, QR_LO, QR_HI)
    plane_out(new, 0, box_out, 1 - right, QR_LO, QR_HI)
    box_out[right, pl.ds(0, 8), :] = segs[0]
    same_out[...] = box_out[0]
    other_out[...] = box_out[1]


def segments_kernel(seg, from_dn, frame):
    frame[0] = jnp.zeros((8, 128), F32)
    frame[0, pl.ds(0, 1), :] = from_dn[pl.ds(SEG_ROW, 1), :]
    frame[0, pl.ds(1, 4), :] = seg[0].astype(F32)


def qr_kernel(field, same, other, seg, prolongator, coarse, box):
    box[0] = same[...]
    box[1] = other[...]
    right = parity()
    lane = lax.broadcasted_iota(jnp.int32, (8, 128), 1)
    even = lane % 2 == 0
    valid_row = lax.broadcasted_iota(jnp.int32, (8, 128), 0) < 5

    def planes(fx):
        if fx == 0:
            return [lambda i, r: far(1 - right, i, r), lambda i, r: near(0, i, r)]
        return [lambda i, r: near(1, i, r), lambda i, r: far(right, i, r)]

    def near(p, i, row):
        return field[i, p, pl.ds(row, 8, stride=2), :]

    def far(slot, i, row):
        return box[slot, pl.ds(spot(i, row, QR_LO, QR_HI), 8, stride=2), :]

    starts = None
    for fx in range(2):
        ids = seg[0] if fx else box[1 - right, pl.ds(0, 8), :]
        joins_next = (ids == roll_z(ids, -2)) & (lane < 126)
        joins_prev = (ids == roll_z(ids, 2)) & (lane >= 2)

        def total(x):
            x = x + jnp.where(even, roll_z(x, -1), roll_z(x, 1))
            return x + jnp.where(joins_next, roll_z(x, -2), 0.0) + jnp.where(joins_prev, roll_z(x, 2), 0.0)

        def dot(a, b):
            s = a[0] * b[0]
            t = a[1] * b[1]
            u = a[2] * b[2]
            for n in range(3, 12, 3):
                s = s + a[n] * b[n]
                t = t + a[n + 1] * b[n + 1]
                u = u + a[n + 2] * b[n + 2]
            return total(s + t + u)

        if fx == 1:
            slot = lane.astype(F32)
            found = jnp.zeros((8, 128), jnp.int32)
            for bit in (64, 32, 16, 8, 4, 2, 1):
                before = jnp.take_along_axis(ids, found + (bit - 1), axis=1)
                found = jnp.where(before < slot, found + bit, found)
            top = jnp.max(ids, axis=1, keepdims=True)
            starts = found
            in_use = slot <= top

            def put(k, j, values):
                compact = jnp.take_along_axis(values, starts, axis=1)
                compact = jnp.where(in_use, compact, 0.0)
                coarse[k, j, 0] = compact[1:5, 0:NSEG]

        cols = []
        for i in range(K):
            col = []
            for get in planes(fx):
                for first in (7, 8):
                    for d in range(3):
                        col.append(get(i * 3 + d, first))
            cols.append([jnp.where(valid_row, x, 1.0) for x in col])
        for k in range(K):
            length = jnp.sqrt(dot(cols[k], cols[k]))
            scale = 1.0 / length
            cols[k] = [x * scale for x in cols[k]]
            if fx == 1:
                put(k, k, length)
            for j in range(k + 1, K):
                r = dot(cols[k], cols[j])
                cols[j] = [x - r * y for x, y in zip(cols[j], cols[k])]
                if fx == 1:
                    put(k, j, r)
                    coarse[j, k, 0] = jnp.zeros((4, NSEG), F32)
            member = 1 - fx
            for d in range(3):
                odd_first = cols[k][member * 6 + d]
                even_first = cols[k][member * 6 + 3 + d]
                prolongator[k, d, fx, pl.ds(0, 4, stride=2), :] = even_first[0:4]
                prolongator[k, d, fx, pl.ds(1, 4, stride=2), :] = odd_first[1:5]


def moved(block, axis, by):
    size = lax.axis_size(axis)
    return lax.ppermute(block, axis, [((i + by) % size, i) for i in range(size)])


def swapped(same, other):
    size = lax.axis_size("gx")
    pairs = [(i, i + 1) for i in range(0, size, 2)]
    around = [(i, (i + 1) % size) for i in range(1, size, 2)]
    return [
        lax.ppermute(block, "gx", two + [(j, i) for i, j in two])
        for block, two in ((same, pairs), (other, around))
    ]


def body(stencil, cands, seg):
    frame = struct(24, 2, ROWS, 128)
    operator = [struct(117, 2, ROWS, 128), struct(9 * len(ROLLED), 2, ROWS, 128), struct(6, 2, ROWS, 128)]
    rim_dn, rim_up, coef, rolled, inverse, field = call(
        pack_kernel, [struct(RIM, 128)] * 2 + operator + [frame], stencil, cands
    )
    rim_from_up = moved(rim_dn, "gy", 1)
    rim_from_dn = moved(rim_up, "gy", -1)
    halo_dn, halo_up = call(pack_halo_kernel, [struct(HALO, 128)] * 2, stencil, inverse)
    halo_dn, halo_up, rim_from_up, rim_from_dn = lax.optimization_barrier(
        (halo_dn, halo_up, rim_from_up, rim_from_dn)
    )
    halo_from_up = moved(halo_dn, "gy", 1)
    halo_from_dn = moved(halo_up, "gy", -1)

    def side(t):
        return [struct(side_rows(*ROUNDS[t][1:], 24), 128)] * 2

    def box(t, hi=None):
        lo, hi = ROUNDS[t][1:] if t is not None else (QR_LO, QR_HI)
        return pltpu.VMEM((2, side_rows(lo, hi, 24), 128), F32)

    coef, field, same, other = call(
        first_kernel, [operator[0], frame] + side(0), rim_from_up, rim_from_dn, coef, field,
        aliases={2: 0, 3: 1}, scratch=[box(0)],
    )
    for t in range(ITERS):
        same, other = swapped(same, other)
        part = call(functools.partial(local_kernel, ROUNDS[t][0]), [frame], coef, rolled, field, flops=10**7)[0]
        args = (coef, rolled, inverse, field, part, same, other)
        if t == 0:
            edge = struct(EDGE, 128)
            field, to_dn, to_up = call(sweep_first, [frame, edge, edge], *args, seg, scratch=[box(0)])
            from_up = moved(to_dn, "gy", 1)
            from_dn = moved(to_up, "gy", -1)
            segs = call(segments_kernel, [struct(1, 8, 128)], seg, from_dn)[0]
            coef, rolled, inverse = call(
                halo_kernel, operator, halo_from_up, halo_from_dn, coef, rolled, inverse, aliases={2: 0, 3: 1, 4: 2}
            )
            field, same, other = call(
                second_kernel, [frame] + side(1), from_up, from_dn, coef, field,
                aliases={3: 0}, scratch=[box(1)],
            )
        elif t < ITERS - 1:
            field, same, other = call(
                functools.partial(sweep_kernel, t), [frame] + side(t + 1), *args, scratch=[box(t), box(t + 1)]
            )
        else:
            last = struct(side_rows(QR_LO, QR_HI, 24), 128)
            field, same, other = call(
                last_kernel, [frame, last, last], *args, segs, scratch=[box(t), box(None)]
            )
    same, other = swapped(same, other)
    prolongator, coarse = call(
        qr_kernel, [struct(K, 3, 2, 8, 128), struct(K, K, 1, 4, NSEG)], field, same, other, segs,
        scratch=[box(None)],
    )
    return prolongator, coarse


def solution(mesh):
    in_specs = (
        P(None, None, None, "gx", "gy", None),
        P(None, None, "gx", "gy", None),
        P("gx", "gy", None),
    )
    out_specs = (P(None, None, "gx", "gy", None), P(None, None, "gx", "gy", None))
    return jax.shard_map(body, mesh=mesh, in_specs=in_specs, out_specs=out_specs, check_vma=False)
```

```python
import functools

import jax
import jax.numpy as jnp
import numpy as np
from jax import lax
from jax.experimental import pallas as pl
from jax.experimental.pallas import tpu as pltpu
from jax.sharding import PartitionSpec as P

ITERS = 4
NSEG = 63
K = 8
DAMPING = 0.8
F32 = jnp.float32
neighbour_steps = [
    (sx, sy, sz)
    for sx in (-1, 0, 1)
    for sy in (-1, 0, 1)
    for sz in (-1, 0, 1)
    if (sx, sy, sz) > (0, 0, 0)
]
ROLLED = [j for j, o in enumerate(neighbour_steps) if o[2] != 0]
SYM = [(0, 0), (0, 1), (0, 2), (1, 1), (1, 2), (2, 2)]
SYM_OF = {(e, d): SYM.index((min(e, d), max(e, d))) for e in range(3) for d in range(3)}
ROWS = 24
VMEM = pl.BlockSpec(memory_space=pltpu.VMEM)
ANY = pl.BlockSpec(memory_space=pl.ANY)
LIMIT = 12 * 2**20

ONE_DN = [j for j, o in enumerate(neighbour_steps) if o[1] == -1]
ONE_UP = [j for j, o in enumerate(neighbour_steps) if o[1] == 1]
RIM_S = 48
RIM = 160
HALO = 4 * 2 * (6 + 117)
SEG_ROW = 4 * 48
EDGE = SEG_ROW + 8
PAD = 8
FLOPS_PER_US = 1.1e9
BYTES_PER_US = 3.6e6


def call(kernel, out_shape, *args, us=0.3, aliases=None, scratch=(), after=0):
    return pl.pallas_call(
        kernel,
        out_shape=out_shape,
        in_specs=[VMEM] * (len(args) - after) + [ANY] * after,
        out_specs=jax.tree.map(lambda _: VMEM, out_shape),
        input_output_aliases=aliases or {},
        scratch_shapes=list(scratch),
        compiler_params=pltpu.CompilerParams(vmem_limit_bytes=LIMIT),
        cost_estimate=pl.CostEstimate(flops=int(us * FLOPS_PER_US), bytes_accessed=int(us * BYTES_PER_US), transcendentals=0),
    )(*args)


def parity():
    return lax.rem(lax.axis_index("gx"), 2)


def struct(*shape):
    return jax.ShapeDtypeStruct(shape, F32)


def invert(b):
    a00, a01, a02, a11, a12, a22 = b
    c00 = a11 * a22 - a12 * a12
    c01 = a12 * a02 - a01 * a22
    c02 = a01 * a12 - a11 * a02
    c11 = a00 * a22 - a02 * a02
    c12 = a01 * a02 - a00 * a12
    c22 = a00 * a11 - a01 * a01
    det = a00 * c00 + a01 * c01 + a02 * c02
    return [c / det for c in (c00, c01, c02, c11, c12, c22)]


def pack_kernel(stencil, cands, rim_dn, rim_up, coef, rolled, inverse, field):
    own = pl.ds(8, 8)
    for c in range(K):
        for d in range(3):
            field[c * 3 + d, :, own, :] = cands[c, d]
    for p in range(2):
        blocks = [stencil[0, e, d, p] for e, d in SYM]
        for i, entry in enumerate(invert(blocks)):
            inverse[i, p, own, :] = entry
    for j in range(13):
        for e in range(3):
            for d in range(3):
                block = stencil[1 + j, e, d]
                coef[j * 9 + e * 3 + d, :, own, :] = block
                if j in ROLLED:
                    rolled[ROLLED.index(j) * 9 + e * 3 + d, :, own, :] = roll_z(
                        block, neighbour_steps[j][2]
                    )
    for c in range(K):
        for d in range(3):
            for p in range(2):
                i = (c * 3 + d) * 2 + p
                rim_dn[pl.ds(i, 1), :] = cands[c, d, p, 0:1]
                rim_up[pl.ds(i, 1), :] = cands[c, d, p, 7:8]
    for msg, ones, row in ((rim_dn, ONE_DN, 0), (rim_up, ONE_UP, 7)):
        for n, j in enumerate(ones):
            for e in range(3):
                for d in range(3):
                    for p in range(2):
                        at = RIM_S + n * 18 + (e * 3 + d) * 2 + p
                        msg[pl.ds(at, 1), :] = stencil[1 + j, e, d, p, row : row + 1]


def roll_z(x, by):
    return pltpu.roll(x, by % 128, x.ndim - 1)


def pack_halo_kernel(stencil, inverse, _, _2, halo_dn, halo_up):
    for i in range(6):
        for p in range(2):
            k = i * 2 + p
            halo_dn[pl.ds(4 * k, 4), :] = inverse[i, p, pl.ds(8, 4), :]
            halo_up[pl.ds(4 * k, 4), :] = inverse[i, p, pl.ds(12, 4), :]
    for j in range(13):
        for e in range(3):
            for d in range(3):
                for p in range(2):
                    k = 12 + ((j * 3 + e) * 3 + d) * 2 + p
                    halo_dn[pl.ds(4 * k, 4), :] = stencil[1 + j, e, d, p, 0:4]
                    halo_up[pl.ds(4 * k, 4), :] = stencil[1 + j, e, d, p, 4:8]


def halo_kernel(from_up, from_dn, coef_in, rolled_in, inverse_in, coef, rolled, inverse):
    for msg, four in ((from_up, 16), (from_dn, 4)):
        for i in range(6):
            for p in range(2):
                inverse[i, p, pl.ds(four, 4), :] = msg[pl.ds(4 * (2 * i + p), 4), :]
        for j in range(13):
            for n in range(9):
                k = 12 + (j * 9 + n) * 2
                pair = msg[pl.ds(4 * k, 8), :]
                coef[j * 9 + n, 0, pl.ds(four, 4), :] = pair[0:4]
                coef[j * 9 + n, 1, pl.ds(four, 4), :] = pair[4:8]
                if j in ROLLED:
                    pair = roll_z(pair, neighbour_steps[j][2])
                    rolled[ROLLED.index(j) * 9 + n, 0, pl.ds(four, 4), :] = pair[0:4]
                    rolled[ROLLED.index(j) * 9 + n, 1, pl.ds(four, 4), :] = pair[4:8]


def matrices(coef, rolled, far_coef=None, far_rolled=None):
    def get(j, e, d, plane, row, turned):
        n = (ROLLED.index(j) if turned else j) * 9 + e * 3 + d
        if plane >= 0:
            return (rolled if turned else coef)[n, plane, pl.ds(row, 8), :]
        n = (STEP_ROLLED.index(j) if turned else STEP.index(j)) * 9 + e * 3 + d
        return (far_rolled if turned else far_coef)[n, pl.ds(row, 8), :]

    return get


def gather_terms(matrix, load, base, half, terms):
    lane = lax.broadcasted_iota(jnp.int32, (8, 128), 1)
    acc = {}
    loads = {}

    def value(c, d, plane, oy):
        key = (c, d, plane, oy)
        if key not in loads:
            loads[key] = load((half * 4 + c) * 3 + d, plane, base + oy)
        return loads[key]

    def order(term):
        oy = neighbour_steps[term[2]][1]
        return term[1], -oy if term[3] else oy

    for cp, fp, j, transposed in sorted(terms, key=order):
        oy, oz = neighbour_steps[j][1:]
        for d in range(3):
            for e in range(3):
                if transposed:
                    m = matrix(j, d, e, cp, base - oy, False)
                    shift, row = -oz, -oy
                else:
                    m = matrix(j, e, d, cp, base, oz != 0)
                    shift, row = oz, oy
                for c in range(4):
                    t = m * value(c, d, fp, row)
                    key = (c, e, shift)
                    acc[key] = acc[key] + t if key in acc else t
    out = []
    for c in range(4):
        line = []
        for e in range(3):
            total = acc[c, e, 0]
            total = total + jnp.where(lane < 127, roll_z(acc[c, e, 1], -1), 0.0)
            total = total + jnp.where(lane > 0, roll_z(acc[c, e, -1], 1), 0.0)
            line.append(total)
        out.append(line)
    return out


FLAT = [j for j, o in enumerate(neighbour_steps) if o[0] == 0]
STEP = [j for j, o in enumerate(neighbour_steps) if o[0] == 1]
STEP_ROLLED = [j for j in STEP if j in ROLLED]
TERMS = [
    [(0, 0, j, t) for j in FLAT for t in (False, True)] + [(0, 1, j, False) for j in STEP],
    [(1, 1, j, t) for j in FLAT for t in (False, True)] + [(0, 0, j, True) for j in STEP],
]
OUT_TERMS = [(1, 1, j, True) for j in STEP]
IN_TERMS = [(1, 2, j, False) for j in STEP]
LEFT_TERMS = [(-1, -1, j, True) for j in STEP]
FAR_TERMS = [(-1, 0, j, False) for j in STEP]


def from_frame(field):
    return lambda i, plane, row: field[i, plane, pl.ds(row, 8), :]


def tiles(bases, step):
    if len(bases) == 1:
        for half in range(2):
            step(bases[0], half)
        return

    def one(i, carry):
        step(bases[0] + (i // 2) * 8, i % 2)
        return carry

    lax.fori_loop(0, 2 * len(bases), one, 0)


def side_rows(lo, hi, items):
    return PAD + items * (hi - lo) + PAD


def spot(i, row, lo, hi):
    return PAD + i * (hi - lo) + row - lo


def outgoing(coef, field, msg, slot, bases, lo, hi):
    def step(base, half):
        got = gather_terms(matrices(coef, None), from_frame(field), base, half, OUT_TERMS)
        for c in range(4):
            for e in range(3):
                i = (half * 4 + c) * 3 + e
                msg[slot, pl.ds(spot(i, base, lo, hi), 8), :] = got[c][e]

    tiles(bases, step)


def plane_out(field, plane, msg, slot, lo, hi):
    for i in range(24):
        msg[slot, pl.ds(spot(i, lo, lo, hi), hi - lo), :] = field[i, plane, pl.ds(lo, hi - lo), :]


def send(coef, field, box, same, other, bases, lo, hi):
    right = parity()
    outgoing(coef, field, box, right, bases, lo, hi)
    plane_out(field, 0, box, 1 - right, lo, hi)
    same[...] = box[0]
    other[...] = box[1]


def first_kernel(from_up, from_dn, coef_in, field_in, coef, field, same, other, box):
    for msg, row, ones in ((from_up, 16, ONE_DN), (from_dn, 7, ONE_UP)):
        for i in range(24):
            for p in range(2):
                field[i, p, pl.ds(row, 1), :] = msg[pl.ds(2 * i + p, 1), :]
        for m, j in enumerate(ones):
            for n in range(9):
                for p in range(2):
                    at = RIM_S + m * 18 + n * 2 + p
                    coef[j * 9 + n, p, pl.ds(row, 1), :] = msg[pl.ds(at, 1), :]
    send(coef, field, box, same, other, *ROUNDS[0])


def second_kernel(from_up, from_dn, coef, field_in, field, same, other, box):
    for msg, row in ((from_up, 16), (from_dn, 4)):
        for i in range(24):
            for p in range(2):
                field[i, p, pl.ds(row, 4), :] = msg[pl.ds(4 * (2 * i + p), 4), :]
    send(coef, field, box, same, other, *ROUNDS[1])


def both_kernel(lo, hi, field, part, segs, same, other, box):
    right = parity()
    for plane, slot in ((1, right), (0, 1 - right)):
        for i in range(24):
            for n, ref in ((i, field), (24 + i, part)):
                box[slot, pl.ds(spot(n, lo, lo, hi), hi - lo), :] = ref[i, plane, pl.ds(lo, hi - lo), :]
    box[right, pl.ds(0, 8), :] = segs[0]
    same[...] = box[0]
    other[...] = box[1]


def pack_far_kernel(coef, inverse, same, other, box):
    right = parity()
    for i in range(81):
        box[right, pl.ds(16 * i, 16), :] = coef[9 * STEP[0] + i, 1, pl.ds(4, 16), :]
    for i in range(6):
        box[right, pl.ds(16 * (81 + i), 16), :] = inverse[i, 1, pl.ds(4, 16), :]
        box[1 - right, pl.ds(16 * (81 + i), 16), :] = inverse[i, 0, pl.ds(4, 16), :]
    same[...] = box[0]
    other[...] = box[1]


def far_kernel(same, other, far_coef, far_rolled, far_inverse, box):
    box[0] = same[...]
    box[1] = other[...]
    right = parity()
    rows = pl.ds(4, 16)
    for k, j in enumerate(STEP):
        for n in range(9):
            block = box[1 - right, pl.ds(16 * (9 * k + n), 16), :]
            far_coef[9 * k + n, rows, :] = block
            if j in ROLLED:
                far_rolled[9 * STEP_ROLLED.index(j) + n, rows, :] = roll_z(block, neighbour_steps[j][2])
    for i in range(6):
        far_inverse[i, 0, rows, :] = box[1 - right, pl.ds(16 * (81 + i), 16), :]
        far_inverse[i, 1, rows, :] = box[right, pl.ds(16 * (81 + i), 16), :]


def beyond_kernel(bases, coef, far_coef, far_rolled, field, far_part):
    get = matrices(coef, None, far_coef, far_rolled)

    def step(base, half):
        for n, terms in enumerate((FAR_TERMS, OUT_TERMS)):
            got = gather_terms(get, from_frame(field), base, half, terms)
            for c in range(4):
                for e in range(3):
                    far_part[(half * 4 + c) * 3 + e, n, pl.ds(base, 8), :] = got[c][e]

    tiles(bases, step)


def relax(inverse, p, base, v, res):
    inv = [inverse[n, p, pl.ds(base, 8), :] * DAMPING for n in range(6)]
    out = []
    for e in range(3):
        move = inv[SYM_OF[e, 0]] * res[0] + inv[SYM_OF[e, 1]] * res[1] + inv[SYM_OF[e, 2]] * res[2]
        out.append((1.0 - DAMPING) * v[e] - move)
    return out


def four_kernel(lo, hi, bases, coef, rolled, far_coef, inverse, far_inverse, field, part, far_part, same, other, new, far, far_seg, box):
    box[0] = same[...]
    box[1] = other[...]
    right = parity()
    get = matrices(coef, rolled, far_coef)

    far_seg[0] = box[1 - right, pl.ds(0, 8), :]

    def message(side, i, row):
        return box[right if side else 1 - right, pl.ds(spot(i, row, lo, hi), 8), :]

    def load(i, plane, row):
        return message(plane == 2, i, row)

    def step(base, half):
        here = pl.ds(base, 8)
        for p, terms in enumerate((LEFT_TERMS, IN_TERMS)):
            got = gather_terms(get, load, base, half, terms)
            for c in range(4):
                at = (half * 4 + c) * 3
                res = [part[at + e, p, here, :] + got[c][e] for e in range(3)]
                out = relax(inverse, p, base, [field[at + e, p, here, :] for e in range(3)], res)
                for e in range(3):
                    new[at + e, p, here, :] = out[e]
                res = [message(p, 24 + at + e, base) + far_part[at + e, p, here, :] for e in range(3)]
                out = relax(far_inverse, p, base, [message(p, at + e, base) for e in range(3)], res)
                for e in range(3):
                    far[at + e, p, here, :] = out[e]

    tiles(bases, step)


def local_kernel(bases, coef, rolled, field, part):
    def step(base, half):
        for p in range(2):
            got = gather_terms(matrices(coef, rolled), from_frame(field), base, half, TERMS[p])
            for c in range(4):
                for e in range(3):
                    part[(half * 4 + c) * 3 + e, p, pl.ds(base, 8), :] = got[c][e]

    tiles(bases, step)


def finish(coef, rolled, inverse, field, part, same, other, box, new, bases, lo, hi):
    box[0] = same[...]
    box[1] = other[...]
    right = parity()

    def load(i, plane, row):
        return box[right, pl.ds(spot(i, row, lo, hi), 8), :]

    def step(base, half):
        got = gather_terms(matrices(coef, rolled), load, base, half, IN_TERMS)
        for p in range(2):
            for c in range(4):
                at = (half * 4 + c) * 3
                res = []
                for e in range(3):
                    far = got[c][e] if p else box[1 - right, pl.ds(spot(at + e, base, lo, hi), 8), :]
                    res.append(part[at + e, p, pl.ds(base, 8), :] + far)
                out = relax(inverse, p, base, [field[at + e, p, pl.ds(base, 8), :] for e in range(3)], res)
                for e in range(3):
                    new[at + e, p, pl.ds(base, 8), :] = out[e]

    tiles(bases, step)


ROUNDS = [((8,), 7, 17), ((4, 12), 4, 20), ((4, 12), 5, 19)]
ALL = (4, 12)
LO, HI = 6, 18


def sweep_first(coef, rolled, inverse, field, part, same, other, seg, new, to_dn, to_up, box):
    finish(coef, rolled, inverse, field, part, same, other, box, new, *ROUNDS[0])
    for i in range(24):
        for p in range(2):
            to_dn[pl.ds(4 * (2 * i + p), 4), :] = new[i, p, pl.ds(8, 4), :]
            to_up[pl.ds(4 * (2 * i + p), 4), :] = new[i, p, pl.ds(12, 4), :]
    to_up[pl.ds(SEG_ROW, 1), :] = seg[0, 3:4].astype(F32)


def sweep_second(coef, rolled, inverse, field, part, same, other, new, same_out, other_out, box, box_out):
    finish(coef, rolled, inverse, field, part, same, other, box, new, *ROUNDS[1])
    send(coef, new, box_out, same_out, other_out, *ROUNDS[2])


def sweep_third(coef, rolled, inverse, field, part, same, other, new, box):
    finish(coef, rolled, inverse, field, part, same, other, box, new, *ROUNDS[2])


def segments_kernel(seg, from_dn, frame):
    frame[0] = jnp.zeros((8, 128), F32)
    frame[0, pl.ds(0, 1), :] = from_dn[pl.ds(SEG_ROW, 1), :]
    frame[0, pl.ds(1, 4), :] = seg[0].astype(F32)


def qr_kernel(field, far, seg, far_seg, prolongator, coarse):
    lane = lax.broadcasted_iota(jnp.int32, (8, 128), 1)
    even = lane % 2 == 0
    valid_row = lax.broadcasted_iota(jnp.int32, (8, 128), 0) < 5
    numbers = [far_seg[0], seg[0]]
    joins_next = [(ids == roll_z(ids, -2)) & (lane < 126) for ids in numbers]
    joins_prev = [(ids == roll_z(ids, 2)) & (lane >= 2) for ids in numbers]

    def dot(fx, a, b):
        parts = [x * y for x, y in zip(a, b)]
        while len(parts) > 1:
            parts = [x + y for x, y in zip(parts[::2], parts[1::2])] + parts[len(parts) // 2 * 2 :]
        x = parts[0]
        x = x + jnp.where(even, roll_z(x, -1), roll_z(x, 1))
        return x + (
            jnp.where(joins_next[fx], roll_z(x, -2), 0.0) + jnp.where(joins_prev[fx], roll_z(x, 2), 0.0)
        )

    ids = numbers[1]
    slot = lane.astype(F32)
    starts = jnp.zeros((8, 128), jnp.int32)
    for bit in (64, 32, 16, 8, 4, 2, 1):
        before = jnp.take_along_axis(ids, starts + (bit - 1), axis=1)
        starts = jnp.where(before < slot, starts + bit, starts)
    in_use = slot <= jnp.max(ids, axis=1, keepdims=True)

    def put(k, j, values):
        compact = jnp.take_along_axis(values, starts, axis=1)
        coarse[k, j, 0] = jnp.where(in_use, compact, 0.0)[1:5, 0:NSEG]

    cols = []
    for order in (((far, 0), (field, 0)), ((field, 1), (far, 1))):
        cols.append(
            [
                [
                    jnp.where(valid_row, ref[i * 3 + d, p, pl.ds(first, 8, stride=2), :], 1.0)
                    for ref, p in order
                    for first in (7, 8)
                    for d in range(3)
                ]
                for i in range(K)
            ]
        )
    for k in range(K):
        squares = [dot(fx, cols[fx][k], cols[fx][k]) for fx in range(2)]
        for fx in range(2):
            scale = lax.rsqrt(squares[fx])
            cols[fx][k] = [x * scale for x in cols[fx][k]]
        for j in range(k + 1, K):
            for fx in range(2):
                r = dot(fx, cols[fx][k], cols[fx][j])
                cols[fx][j] = [x - r * y for x, y in zip(cols[fx][j], cols[fx][k])]
                if fx == 1:
                    put(k, j, r)
                    coarse[j, k, 0] = jnp.zeros((4, NSEG), F32)
        put(k, k, jnp.sqrt(squares[1]))
        for fx in range(2):
            at = 6 * (1 - fx)
            for d in range(3):
                prolongator[k, d, fx, pl.ds(0, 4, stride=2), :] = cols[fx][k][at + 3 + d][0:4]
                prolongator[k, d, fx, pl.ds(1, 4, stride=2), :] = cols[fx][k][at + d][1:5]


def moved(block, axis, by):
    size = lax.axis_size(axis)
    return lax.ppermute(block, axis, [((i + by) % size, i) for i in range(size)])


def swapped(same, other):
    size = lax.axis_size("gx")
    pairs = [(i, i + 1) for i in range(0, size, 2)]
    around = [(i, (i + 1) % size) for i in range(1, size, 2)]
    return [
        lax.ppermute(block, "gx", two + [(j, i) for i, j in two])
        for block, two in ((same, pairs), (other, around))
    ]


def body(stencil, cands, seg):
    frame = struct(24, 2, ROWS, 128)
    operator = [struct(117, 2, ROWS, 128), struct(9 * len(ROLLED), 2, ROWS, 128), struct(6, 2, ROWS, 128)]
    rim_dn, rim_up, coef, rolled, inverse, field = call(
        pack_kernel, [struct(RIM, 128)] * 2 + operator + [frame], stencil, cands
    )
    rim_from_up = moved(rim_dn, "gy", 1)
    rim_from_dn = moved(rim_up, "gy", -1)

    edge = struct(EDGE, 128)
    sides = [struct(side_rows(lo, hi, 24), 128) for _, lo, hi in ROUNDS]
    boxes = [pltpu.VMEM((2, *side.shape), F32) for side in sides]

    def local(t):
        bases = ROUNDS[t][0] if t < 3 else ALL
        return call(functools.partial(local_kernel, bases), [frame], coef, rolled, field, us=1.7 if t else 0.9)[0]

    coef, field, same, other = call(
        first_kernel, [operator[0], frame, sides[0], sides[0]], rim_from_up, rim_from_dn, coef, field,
        aliases={2: 0, 3: 1}, scratch=boxes[:1],
    )
    same, other = swapped(same, other)
    halo_dn, halo_up = call(
        pack_halo_kernel, [struct(HALO, 128)] * 2, stencil, inverse, rim_from_up, rim_from_dn, after=2
    )
    halo_from_up = moved(halo_dn, "gy", 1)
    halo_from_dn = moved(halo_up, "gy", -1)
    part = local(0)
    field, to_dn, to_up = call(
        sweep_first, [frame, edge, edge], coef, rolled, inverse, field, part, same, other, seg, scratch=boxes[:1]
    )
    from_up = moved(to_dn, "gy", 1)
    from_dn = moved(to_up, "gy", -1)
    segs = call(segments_kernel, [struct(1, 8, 128)], seg, from_dn)[0]
    coef, rolled, inverse = call(
        halo_kernel, operator, halo_from_up, halo_from_dn, coef, rolled, inverse,
        aliases={2: 0, 3: 1, 4: 2},
    )
    field, same, other = call(
        second_kernel, [frame, sides[1], sides[1]], from_up, from_dn, coef, field, aliases={3: 0}, scratch=boxes[1:2], us=0.6
    )
    same, other = swapped(same, other)
    part = local(1)
    across = struct(16 * 87, 128)
    across_box = pltpu.VMEM((2, *across.shape), F32)
    across_same, across_other = swapped(
        *call(pack_far_kernel, [across, across], coef, inverse, scratch=[across_box])
    )
    field, same, other = call(
        sweep_second, [frame, sides[2], sides[2]], coef, rolled, inverse, field, part, same, other, scratch=boxes[1:], us=1.3
    )
    same, other = swapped(same, other)
    part = local(2)
    far_coef, far_rolled, far_inverse = call(
        far_kernel,
        [struct(81, ROWS, 128), struct(9 * len(STEP_ROLLED), ROWS, 128), operator[2]],
        across_same, across_other, scratch=[across_box],
    )
    field = call(
        sweep_third, [frame], coef, rolled, inverse, field, part, same, other, scratch=boxes[2:], us=0.8
    )[0]
    part = local(3)
    side = struct(side_rows(LO, HI, 48), 128)
    box = pltpu.VMEM((2, *side.shape), F32)
    same, other = swapped(
        *call(functools.partial(both_kernel, LO, HI), [side, side], field, part, segs, scratch=[box])
    )
    far_part = call(
        functools.partial(beyond_kernel, ALL), [frame], coef, far_coef, far_rolled, field, us=0.8
    )[0]
    field, far, far_seg = call(
        functools.partial(four_kernel, LO, HI, ALL), [frame, frame, struct(1, 8, 128)],
        coef, rolled, far_coef, inverse, far_inverse, field, part, far_part, same, other, scratch=[box],
    )
    prolongator, coarse = call(
        qr_kernel, [struct(K, 3, 2, 8, 128), struct(K, K, 1, 4, NSEG)], field, far, segs, far_seg, us=3.0
    )
    return prolongator, coarse


def solution(mesh):
    in_specs = (
        P(None, None, None, "gx", "gy", None),
        P(None, None, "gx", "gy", None),
        P("gx", "gy", None),
    )
    out_specs = (P(None, None, "gx", "gy", None), P(None, None, "gx", "gy", None))
    return jax.shard_map(body, mesh=mesh, in_specs=in_specs, out_specs=out_specs, check_vma=False)
```

```python
import functools

import jax
import jax.numpy as jnp
import numpy as np
from jax import lax
from jax.experimental import pallas as pl
from jax.experimental.pallas import tpu as pltpu
from jax.sharding import PartitionSpec as P

ITERS = 4
NSEG = 63
K = 8
DAMPING = 0.8
F32 = jnp.float32
neighbour_steps = [
    (sx, sy, sz)
    for sx in (-1, 0, 1)
    for sy in (-1, 0, 1)
    for sz in (-1, 0, 1)
    if (sx, sy, sz) > (0, 0, 0)
]
ROLLED = [j for j, o in enumerate(neighbour_steps) if o[2] != 0]
FLAT = [j for j, o in enumerate(neighbour_steps) if o[0] == 0]
STEP = [j for j, o in enumerate(neighbour_steps) if o[0] == 1]
STEP_ROLLED = [j for j in STEP if j in ROLLED]
SYM = [(0, 0), (0, 1), (0, 2), (1, 1), (1, 2), (2, 2)]
SYM_OF = {(e, d): SYM.index((min(e, d), max(e, d))) for e in range(3) for d in range(3)}
ROWS = 24
VMEM = pl.BlockSpec(memory_space=pltpu.VMEM)
ANY = pl.BlockSpec(memory_space=pl.ANY)
LIMIT = 12 * 2**20

ONE_DN = [j for j, o in enumerate(neighbour_steps) if o[1] == -1]
ONE_UP = [j for j, o in enumerate(neighbour_steps) if o[1] == 1]
RIM_S = 48
RIM = 160
SEG_ROW = 4 * 48
EDGE = SEG_ROW + 8
PAD = 8
FLOPS_PER_US = 1.1e9
BYTES_PER_US = 3.6e6


def call(kernel, out_shape, *args, us=0.3, aliases=None, scratch=(), after=0):
    return pl.pallas_call(
        kernel,
        out_shape=out_shape,
        in_specs=[VMEM] * (len(args) - after) + [ANY] * after,
        out_specs=jax.tree.map(lambda _: VMEM, out_shape),
        input_output_aliases=aliases or {},
        scratch_shapes=list(scratch),
        compiler_params=pltpu.CompilerParams(vmem_limit_bytes=LIMIT),
        cost_estimate=pl.CostEstimate(flops=int(us * FLOPS_PER_US), bytes_accessed=int(us * BYTES_PER_US), transcendentals=0),
    )(*args)


def parity():
    return lax.rem(lax.axis_index("gx"), 2)


def struct(*shape):
    return jax.ShapeDtypeStruct(shape, F32)


def invert(b):
    a00, a01, a02, a11, a12, a22 = b
    c00 = a11 * a22 - a12 * a12
    c01 = a12 * a02 - a01 * a22
    c02 = a01 * a12 - a11 * a02
    c11 = a00 * a22 - a02 * a02
    c12 = a01 * a02 - a00 * a12
    c22 = a00 * a11 - a01 * a01
    det = a00 * c00 + a01 * c01 + a02 * c02
    return [c / det for c in (c00, c01, c02, c11, c12, c22)]


def pack_kernel(stencil, cands, rim_dn, rim_up, coef, rolled, inverse, field):
    own = pl.ds(8, 8)
    for c in range(K):
        for d in range(3):
            field[c * 3 + d, :, own, :] = cands[c, d]
    for p in range(2):
        blocks = [stencil[0, e, d, p] for e, d in SYM]
        for i, entry in enumerate(invert(blocks)):
            inverse[i, p, own, :] = entry
    for j in range(13):
        for e in range(3):
            for d in range(3):
                block = stencil[1 + j, e, d]
                coef[j * 9 + e * 3 + d, :, own, :] = block
                if j in ROLLED:
                    rolled[ROLLED.index(j) * 9 + e * 3 + d, :, own, :] = roll_z(
                        block, neighbour_steps[j][2]
                    )
    for c in range(K):
        for d in range(3):
            for p in range(2):
                i = (c * 3 + d) * 2 + p
                rim_dn[pl.ds(i, 1), :] = cands[c, d, p, 0:1]
                rim_up[pl.ds(i, 1), :] = cands[c, d, p, 7:8]
    for msg, ones, row in ((rim_dn, ONE_DN, 0), (rim_up, ONE_UP, 7)):
        for n, j in enumerate(ones):
            for e in range(3):
                for d in range(3):
                    for p in range(2):
                        at = RIM_S + n * 18 + (e * 3 + d) * 2 + p
                        msg[pl.ds(at, 1), :] = stencil[1 + j, e, d, p, row : row + 1]


def roll_z(x, by):
    return pltpu.roll(x, by % 128, x.ndim - 1)


HALO_A = [(j, n, 1) for j in STEP for n in range(9)]
HALO_B = (
    [(None, i, p) for i in range(6) for p in range(2)]
    + [(j, n, p) for j in FLAT for n in range(9) for p in range(2)]
    + [(j, n, 0) for j in STEP for n in range(9)]
)


def halo_shape(items):
    return struct(-(-4 * len(items) // 8) * 8, 128)


def pack_halo_kernel(items, stencil, inverse, halo_dn, halo_up):
    for k, (j, n, p) in enumerate(items):
        rows = pl.ds(4 * k, 4)
        if j is None:
            halo_dn[rows, :] = inverse[n, p, pl.ds(8, 4), :]
            halo_up[rows, :] = inverse[n, p, pl.ds(12, 4), :]
        else:
            halo_dn[rows, :] = stencil[1 + j, n // 3, n % 3, p, 0:4]
            halo_up[rows, :] = stencil[1 + j, n // 3, n % 3, p, 4:8]


def halo_rows(items, from_up, from_dn, coef, rolled, inverse):
    for msg, four in ((from_up, 16), (from_dn, 4)):
        for k, (j, n, p) in enumerate(items):
            block = msg[pl.ds(4 * k, 4), :]
            if j is None:
                inverse[n, p, pl.ds(four, 4), :] = block
                continue
            coef[j * 9 + n, p, pl.ds(four, 4), :] = block
            if j in ROLLED:
                at = ROLLED.index(j) * 9 + n
                rolled[at, p, pl.ds(four, 4), :] = roll_z(block, neighbour_steps[j][2])


def halo_a_kernel(from_up, from_dn, coef_in, rolled_in, coef, rolled):
    halo_rows(HALO_A, from_up, from_dn, coef, rolled, None)


def halo_b_kernel(from_up, from_dn, coef_in, rolled_in, inverse_in, _, coef, rolled, inverse):
    halo_rows(HALO_B, from_up, from_dn, coef, rolled, inverse)


def matrices(coef, rolled, far_coef=None, far_rolled=None):
    def get(j, e, d, plane, row, turned):
        n = (ROLLED.index(j) if turned else j) * 9 + e * 3 + d
        if plane >= 0:
            return (rolled if turned else coef)[n, plane, pl.ds(row, 8), :]
        n = (STEP_ROLLED.index(j) if turned else STEP.index(j)) * 9 + e * 3 + d
        return (far_rolled if turned else far_coef)[n, pl.ds(row, 8), :]

    return get


def gather_terms(matrix, load, base, half, terms):
    lane = lax.broadcasted_iota(jnp.int32, (8, 128), 1)
    acc = {}
    loads = {}

    def value(c, d, plane, oy):
        key = (c, d, plane, oy)
        if key not in loads:
            loads[key] = load((half * 4 + c) * 3 + d, plane, base + oy)
        return loads[key]

    def order(term):
        oy = neighbour_steps[term[2]][1]
        return term[1], -oy if term[3] else oy

    for cp, fp, j, transposed in sorted(terms, key=order):
        oy, oz = neighbour_steps[j][1:]
        for d in range(3):
            for e in range(3):
                if transposed:
                    m = matrix(j, d, e, cp, base - oy, False)
                    shift, row = -oz, -oy
                else:
                    m = matrix(j, e, d, cp, base, oz != 0)
                    shift, row = oz, oy
                for c in range(4):
                    t = m * value(c, d, fp, row)
                    key = (c, e, shift)
                    acc[key] = acc[key] + t if key in acc else t
    out = []
    for c in range(4):
        line = []
        for e in range(3):
            total = acc[c, e, 0]
            total = total + jnp.where(lane < 127, roll_z(acc[c, e, 1], -1), 0.0)
            total = total + jnp.where(lane > 0, roll_z(acc[c, e, -1], 1), 0.0)
            line.append(total)
        out.append(line)
    return out


TERMS = [
    [(0, 0, j, t) for j in FLAT for t in (False, True)] + [(0, 1, j, False) for j in STEP],
    [(1, 1, j, t) for j in FLAT for t in (False, True)] + [(0, 0, j, True) for j in STEP],
]
OUT_TERMS = [(1, 1, j, True) for j in STEP]
IN_TERMS = [(1, 2, j, False) for j in STEP]
LEFT_TERMS = [(-1, -1, j, True) for j in STEP]
FAR_TERMS = [(-1, 0, j, False) for j in STEP]


def from_frame(field):
    return lambda i, plane, row: field[i, plane, pl.ds(row, 8), :]


def tiles(bases, step):
    if len(bases) == 1:
        for half in range(2):
            step(bases[0], half)
        return

    def one(i, carry):
        step(bases[0] + (i // 2) * 8, i % 2)
        return carry

    lax.fori_loop(0, 2 * len(bases), one, 0)


def side_rows(lo, hi, items):
    return PAD + items * (hi - lo) + PAD


def spot(i, row, lo, hi):
    return PAD + i * (hi - lo) + row - lo


def outgoing(coef, field, msg, slot, bases, lo, hi):
    def step(base, half):
        got = gather_terms(matrices(coef, None), from_frame(field), base, half, OUT_TERMS)
        for c in range(4):
            for e in range(3):
                i = (half * 4 + c) * 3 + e
                msg[slot, pl.ds(spot(i, base, lo, hi), 8), :] = got[c][e]

    tiles(bases, step)


def plane_out(field, plane, msg, slot, lo, hi):
    for i in range(24):
        msg[slot, pl.ds(spot(i, lo, lo, hi), hi - lo), :] = field[i, plane, pl.ds(lo, hi - lo), :]


def send(coef, field, box, same, other, bases, lo, hi):
    right = parity()
    outgoing(coef, field, box, right, bases, lo, hi)
    plane_out(field, 0, box, 1 - right, lo, hi)
    same[...] = box[0]
    other[...] = box[1]


def first_kernel(from_up, from_dn, coef_in, field_in, coef, field, same, other, box):
    for msg, row, ones in ((from_up, 16, ONE_DN), (from_dn, 7, ONE_UP)):
        for i in range(24):
            for p in range(2):
                field[i, p, pl.ds(row, 1), :] = msg[pl.ds(2 * i + p, 1), :]
        for m, j in enumerate(ones):
            for n in range(9):
                for p in range(2):
                    at = RIM_S + m * 18 + n * 2 + p
                    coef[j * 9 + n, p, pl.ds(row, 1), :] = msg[pl.ds(at, 1), :]
    send(coef, field, box, same, other, *ROUNDS[0])


def second_kernel(from_up, from_dn, coef, field_in, field, same, other, box):
    for msg, row in ((from_up, 16), (from_dn, 4)):
        for i in range(24):
            for p in range(2):
                field[i, p, pl.ds(row, 4), :] = msg[pl.ds(4 * (2 * i + p), 4), :]
    send(coef, field, box, same, other, *ROUNDS[1])


def both_kernel(lo, hi, field, part, segs, same, other, box):
    right = parity()
    for plane, slot in ((1, right), (0, 1 - right)):
        for i in range(24):
            for n, ref in ((i, field), (24 + i, part)):
                box[slot, pl.ds(spot(n, lo, lo, hi), hi - lo), :] = ref[i, plane, pl.ds(lo, hi - lo), :]
    box[right, pl.ds(0, 8), :] = segs[0]
    same[...] = box[0]
    other[...] = box[1]


def pack_far_kernel(coef, inverse, same, other, box):
    right = parity()
    for i in range(81):
        box[right, pl.ds(TALL * i, TALL), :] = coef[9 * STEP[0] + i, 1, pl.ds(LO, TALL), :]
    for i in range(6):
        box[right, pl.ds(TALL * (81 + i), TALL), :] = inverse[i, 1, pl.ds(LO, TALL), :]
        box[1 - right, pl.ds(TALL * (81 + i), TALL), :] = inverse[i, 0, pl.ds(LO, TALL), :]
    same[...] = box[0]
    other[...] = box[1]


def far_kernel(same, other, far_coef, far_rolled, far_inverse, box):
    box[0] = same[...]
    box[1] = other[...]
    right = parity()
    rows = pl.ds(LO, TALL)
    for k, j in enumerate(STEP):
        for n in range(9):
            block = box[1 - right, pl.ds(TALL * (9 * k + n), TALL), :]
            far_coef[9 * k + n, rows, :] = block
            if j in ROLLED:
                far_rolled[9 * STEP_ROLLED.index(j) + n, rows, :] = roll_z(block, neighbour_steps[j][2])
    for i in range(6):
        far_inverse[i, 0, rows, :] = box[1 - right, pl.ds(TALL * (81 + i), TALL), :]
        far_inverse[i, 1, rows, :] = box[right, pl.ds(TALL * (81 + i), TALL), :]


def beyond_kernel(bases, coef, far_coef, far_rolled, field, far_part):
    get = matrices(coef, None, far_coef, far_rolled)

    def step(base, half):
        for n, terms in enumerate((FAR_TERMS, OUT_TERMS)):
            got = gather_terms(get, from_frame(field), base, half, terms)
            for c in range(4):
                for e in range(3):
                    far_part[(half * 4 + c) * 3 + e, n, pl.ds(base, 8), :] = got[c][e]

    tiles(bases, step)


def relax(inverse, p, base, v, res):
    inv = [inverse[n, p, pl.ds(base, 8), :] * DAMPING for n in range(6)]
    out = []
    for e in range(3):
        move = inv[SYM_OF[e, 0]] * res[0] + inv[SYM_OF[e, 1]] * res[1] + inv[SYM_OF[e, 2]] * res[2]
        out.append((1.0 - DAMPING) * v[e] - move)
    return out


def four_kernel(lo, hi, bases, coef, rolled, far_coef, inverse, far_inverse, field, part, far_part, same, other, new, far, far_seg, box):
    box[0] = same[...]
    box[1] = other[...]
    right = parity()
    get = matrices(coef, rolled, far_coef)

    far_seg[0] = box[1 - right, pl.ds(0, 8), :]

    def message(side, i, row):
        return box[right if side else 1 - right, pl.ds(spot(i, row, lo, hi), 8), :]

    def load(i, plane, row):
        return message(plane == 2, i, row)

    def step(base, half):
        here = pl.ds(base, 8)
        for p, terms in enumerate((LEFT_TERMS, IN_TERMS)):
            got = gather_terms(get, load, base, half, terms)
            for c in range(4):
                at = (half * 4 + c) * 3
                res = [part[at + e, p, here, :] + got[c][e] for e in range(3)]
                out = relax(inverse, p, base, [field[at + e, p, here, :] for e in range(3)], res)
                for e in range(3):
                    new[at + e, p, here, :] = out[e]
                res = [message(p, 24 + at + e, base) + far_part[at + e, p, here, :] for e in range(3)]
                out = relax(far_inverse, p, base, [message(p, at + e, base) for e in range(3)], res)
                for e in range(3):
                    far[at + e, p, here, :] = out[e]

    tiles(bases, step)


def local_kernel(bases, coef, rolled, field, part):
    def step(base, half):
        for p in range(2):
            got = gather_terms(matrices(coef, rolled), from_frame(field), base, half, TERMS[p])
            for c in range(4):
                for e in range(3):
                    part[(half * 4 + c) * 3 + e, p, pl.ds(base, 8), :] = got[c][e]

    tiles(bases, step)


def finish(coef, rolled, inverse, field, part, same, other, box, new, bases, lo, hi):
    box[0] = same[...]
    box[1] = other[...]
    right = parity()

    def load(i, plane, row):
        return box[right, pl.ds(spot(i, row, lo, hi), 8), :]

    def step(base, half):
        got = gather_terms(matrices(coef, rolled), load, base, half, IN_TERMS)
        for p in range(2):
            for c in range(4):
                at = (half * 4 + c) * 3
                res = []
                for e in range(3):
                    far = got[c][e] if p else box[1 - right, pl.ds(spot(at + e, base, lo, hi), 8), :]
                    res.append(part[at + e, p, pl.ds(base, 8), :] + far)
                out = relax(inverse, p, base, [field[at + e, p, pl.ds(base, 8), :] for e in range(3)], res)
                for e in range(3):
                    new[at + e, p, pl.ds(base, 8), :] = out[e]

    tiles(bases, step)


ROUNDS = [((8,), 7, 17), ((4, 12), 4, 20), ((4, 12), 5, 19)]
ALL = (4, 12)
LO, HI = 6, 18
TALL = HI - LO


def sweep_first(coef, rolled, inverse, field, part, same, other, seg, new, to_dn, to_up, box):
    finish(coef, rolled, inverse, field, part, same, other, box, new, *ROUNDS[0])
    for i in range(24):
        for p in range(2):
            to_dn[pl.ds(4 * (2 * i + p), 4), :] = new[i, p, pl.ds(8, 4), :]
            to_up[pl.ds(4 * (2 * i + p), 4), :] = new[i, p, pl.ds(12, 4), :]
    to_up[pl.ds(SEG_ROW, 1), :] = seg[0, 3:4].astype(F32)


def sweep_second(coef, rolled, inverse, field, part, same, other, new, same_out, other_out, box, box_out):
    finish(coef, rolled, inverse, field, part, same, other, box, new, *ROUNDS[1])
    send(coef, new, box_out, same_out, other_out, *ROUNDS[2])


def sweep_third(coef, rolled, inverse, field, part, same, other, new, box):
    finish(coef, rolled, inverse, field, part, same, other, box, new, *ROUNDS[2])


def segments_kernel(seg, from_dn, frame):
    frame[0] = jnp.zeros((8, 128), F32)
    frame[0, pl.ds(0, 1), :] = from_dn[pl.ds(SEG_ROW, 1), :]
    frame[0, pl.ds(1, 4), :] = seg[0].astype(F32)


def qr_kernel(field, far, seg, far_seg, prolongator, coarse):
    lane = lax.broadcasted_iota(jnp.int32, (8, 128), 1)
    valid_row = lax.broadcasted_iota(jnp.int32, (8, 128), 0) < 5
    numbers = [far_seg[0], seg[0]]
    joins = [
        [(by, (ids == roll_z(ids, -by)) & (lane + by >= 0) & (lane + by < 128)) for by in (-3, -2, -1, 1, 2, 3)]
        for ids in numbers
    ]

    def dot(fx, a, b):
        parts = [x * y for x, y in zip(a, b)]
        while len(parts) > 1:
            parts = [x + y for x, y in zip(parts[::2], parts[1::2])] + parts[len(parts) // 2 * 2 :]
        x = parts[0]
        a, b, c, d, e, f = [jnp.where(mask, roll_z(x, -by), 0.0) for by, mask in joins[fx]]
        return ((x + a) + (b + c)) + ((d + e) + f)

    ids = numbers[1]
    slot = lane.astype(F32)
    starts = jnp.zeros((8, 128), jnp.int32)
    for bit in (64, 32, 16, 8, 4, 2, 1):
        before = jnp.take_along_axis(ids, starts + (bit - 1), axis=1)
        starts = jnp.where(before < slot, starts + bit, starts)
    in_use = slot <= jnp.max(ids, axis=1, keepdims=True)

    def put(k, j, values):
        compact = jnp.take_along_axis(values, starts, axis=1)
        coarse[k, j, 0] = jnp.where(in_use, compact, 0.0)[1:5, 0:NSEG]

    cols = []
    for order in (((far, 0), (field, 0)), ((field, 1), (far, 1))):
        cols.append(
            [
                [
                    jnp.where(valid_row, ref[i * 3 + d, p, pl.ds(first, 8, stride=2), :], 1.0)
                    for ref, p in order
                    for first in (7, 8)
                    for d in range(3)
                ]
                for i in range(K)
            ]
        )
    for k in range(K):
        squares = [dot(fx, cols[fx][k], cols[fx][k]) for fx in range(2)]
        for fx in range(2):
            scale = lax.rsqrt(squares[fx])
            cols[fx][k] = [x * scale for x in cols[fx][k]]
        for j in range(k + 1, K):
            for fx in range(2):
                r = dot(fx, cols[fx][k], cols[fx][j])
                cols[fx][j] = [x - r * y for x, y in zip(cols[fx][j], cols[fx][k])]
                if fx == 1:
                    put(k, j, r)
                    coarse[j, k, 0] = jnp.zeros((4, NSEG), F32)
        put(k, k, jnp.sqrt(squares[1]))
        for fx in range(2):
            at = 6 * (1 - fx)
            for d in range(3):
                prolongator[k, d, fx, pl.ds(0, 4, stride=2), :] = cols[fx][k][at + 3 + d][0:4]
                prolongator[k, d, fx, pl.ds(1, 4, stride=2), :] = cols[fx][k][at + d][1:5]


def moved(block, axis, by):
    size = lax.axis_size(axis)
    return lax.ppermute(block, axis, [((i + by) % size, i) for i in range(size)])


def swapped(same, other):
    size = lax.axis_size("gx")
    pairs = [(i, i + 1) for i in range(0, size, 2)]
    around = [(i, (i + 1) % size) for i in range(1, size, 2)]
    return [
        lax.ppermute(block, "gx", two + [(j, i) for i, j in two])
        for block, two in ((same, pairs), (other, around))
    ]


def body(stencil, cands, seg):
    frame = struct(24, 2, ROWS, 128)
    operator = [struct(117, 2, ROWS, 128), struct(9 * len(ROLLED), 2, ROWS, 128), struct(6, 2, ROWS, 128)]
    rim_dn, rim_up, coef, rolled, inverse, field = call(
        pack_kernel, [struct(RIM, 128)] * 2 + operator + [frame], stencil, cands
    )
    rim_from_up = moved(rim_dn, "gy", 1)
    rim_from_dn = moved(rim_up, "gy", -1)

    edge = struct(EDGE, 128)
    sides = [struct(side_rows(lo, hi, 24), 128) for _, lo, hi in ROUNDS]
    boxes = [pltpu.VMEM((2, *side.shape), F32) for side in sides]

    def local(t):
        bases = ROUNDS[t][0] if t < 3 else ALL
        return call(functools.partial(local_kernel, bases), [frame], coef, rolled, field, us=1.7 if t else 0.9)[0]

    coef, field, same, other = call(
        first_kernel, [operator[0], frame, sides[0], sides[0]], rim_from_up, rim_from_dn, coef, field,
        aliases={2: 0, 3: 1}, scratch=boxes[:1],
    )
    same, other = swapped(same, other)
    halo = []
    for items in (HALO_A, HALO_B):
        halo_dn, halo_up = call(
            functools.partial(pack_halo_kernel, items), [halo_shape(items)] * 2, stencil, inverse, us=0.1
        )
        halo.append((moved(halo_dn, "gy", 1), moved(halo_up, "gy", -1)))
    part = local(0)
    field, to_dn, to_up = call(
        sweep_first, [frame, edge, edge], coef, rolled, inverse, field, part, same, other, seg, scratch=boxes[:1], us=4
    )
    from_up = moved(to_dn, "gy", 1)
    from_dn = moved(to_up, "gy", -1)
    segs = call(segments_kernel, [struct(1, 8, 128)], seg, from_dn)[0]
    coef, rolled = call(halo_a_kernel, operator[:2], *halo[0], coef, rolled, aliases={2: 0, 3: 1})
    field, same, other = call(
        second_kernel, [frame, sides[1], sides[1]], from_up, from_dn, coef, field,
        aliases={3: 0}, scratch=boxes[1:2], us=3,
    )
    coef, rolled, inverse = call(
        halo_b_kernel, operator, *halo[1], coef, rolled, inverse, field, aliases={2: 0, 3: 1, 4: 2}, after=1
    )
    same, other = swapped(same, other)
    part = local(1)
    across = struct(-(-TALL * 87 // 8) * 8, 128)
    across_box = pltpu.VMEM((2, *across.shape), F32)
    across_same, across_other = swapped(
        *call(pack_far_kernel, [across, across], coef, inverse, scratch=[across_box])
    )
    field, same, other = call(
        sweep_second, [frame, sides[2], sides[2]], coef, rolled, inverse, field, part, same, other, scratch=boxes[1:], us=1.3
    )
    same, other = swapped(same, other)
    part = local(2)
    far_coef, far_rolled, far_inverse = call(
        far_kernel,
        [struct(81, ROWS, 128), struct(9 * len(STEP_ROLLED), ROWS, 128), operator[2]],
        across_same, across_other, scratch=[across_box],
    )
    field = call(
        sweep_third, [frame], coef, rolled, inverse, field, part, same, other, scratch=boxes[2:], us=0.8
    )[0]
    part = local(3)
    side = struct(side_rows(LO, HI, 48), 128)
    box = pltpu.VMEM((2, *side.shape), F32)
    same, other = swapped(
        *call(functools.partial(both_kernel, LO, HI), [side, side], field, part, segs, scratch=[box])
    )
    far_part = call(
        functools.partial(beyond_kernel, ALL), [frame], coef, far_coef, far_rolled, field, us=0.8
    )[0]
    field, far, far_seg = call(
        functools.partial(four_kernel, LO, HI, ALL), [frame, frame, struct(1, 8, 128)],
        coef, rolled, far_coef, inverse, far_inverse, field, part, far_part, same, other, scratch=[box],
    )
    prolongator, coarse = call(
        qr_kernel, [struct(K, 3, 2, 8, 128), struct(K, K, 1, 4, NSEG)], field, far, segs, far_seg, us=3.0
    )
    return prolongator, coarse


def solution(mesh):
    in_specs = (
        P(None, None, None, "gx", "gy", None),
        P(None, None, "gx", "gy", None),
        P("gx", "gy", None),
    )
    out_specs = (P(None, None, "gx", "gy", None), P(None, None, "gx", "gy", None))
    return jax.shard_map(body, mesh=mesh, in_specs=in_specs, out_specs=out_specs, check_vma=False)
```

```python
import functools

import jax
import jax.numpy as jnp
import numpy as np
from jax import lax
from jax.experimental import pallas as pl
from jax.experimental.pallas import tpu as pltpu
from jax.sharding import PartitionSpec as P

ITERS = 4
NSEG = 63
K = 8
DAMPING = 0.8
F32 = jnp.float32
neighbour_steps = [
    (sx, sy, sz)
    for sx in (-1, 0, 1)
    for sy in (-1, 0, 1)
    for sz in (-1, 0, 1)
    if (sx, sy, sz) > (0, 0, 0)
]
ROLLED = [j for j, o in enumerate(neighbour_steps) if o[2] != 0]
FLAT = [j for j, o in enumerate(neighbour_steps) if o[0] == 0]
STEP = [j for j, o in enumerate(neighbour_steps) if o[0] == 1]
STEP_ROLLED = [j for j in STEP if j in ROLLED]
SYM = [(0, 0), (0, 1), (0, 2), (1, 1), (1, 2), (2, 2)]
SYM_OF = {(e, d): SYM.index((min(e, d), max(e, d))) for e in range(3) for d in range(3)}
ROWS = 24
VMEM = pl.BlockSpec(memory_space=pltpu.VMEM)
ANY = pl.BlockSpec(memory_space=pl.ANY)
LIMIT = 12 * 2**20

ONE_DN = [j for j, o in enumerate(neighbour_steps) if o[1] == -1]
ONE_UP = [j for j, o in enumerate(neighbour_steps) if o[1] == 1]
RIM_S = 48
RIM = 160
SEG_ROW = 4 * 48
EDGE = SEG_ROW + 8
PAD = 8
LO, HI = 6, 18
TALL = HI - LO
FLOPS_PER_US = 1.1e9
BYTES_PER_US = 3.6e6


def call(kernel, out_shape, *args, us=0.3, aliases=None, scratch=(), after=0):
    return pl.pallas_call(
        kernel,
        out_shape=out_shape,
        in_specs=[VMEM] * (len(args) - after) + [ANY] * after,
        out_specs=jax.tree.map(lambda _: VMEM, out_shape),
        input_output_aliases=aliases or {},
        scratch_shapes=list(scratch),
        compiler_params=pltpu.CompilerParams(vmem_limit_bytes=LIMIT),
        cost_estimate=pl.CostEstimate(flops=int(us * FLOPS_PER_US), bytes_accessed=int(us * BYTES_PER_US), transcendentals=0),
    )(*args)


def parity():
    return lax.rem(lax.axis_index("gx"), 2)


def struct(*shape):
    return jax.ShapeDtypeStruct(shape, F32)


def invert(b):
    a00, a01, a02, a11, a12, a22 = b
    c00 = a11 * a22 - a12 * a12
    c01 = a12 * a02 - a01 * a22
    c02 = a01 * a12 - a11 * a02
    c11 = a00 * a22 - a02 * a02
    c12 = a01 * a02 - a00 * a12
    c22 = a00 * a11 - a01 * a01
    det = a00 * c00 + a01 * c01 + a02 * c02
    return [c / det for c in (c00, c01, c02, c11, c12, c22)]


def pack_kernel(stencil, cands, rim_dn, rim_up, coef, rolled, inverse, field):
    own = pl.ds(8, 8)
    for c in range(K):
        for d in range(3):
            field[c * 3 + d, :, own, :] = cands[c, d]
    for p in range(2):
        blocks = [stencil[0, e, d, p] for e, d in SYM]
        for i, entry in enumerate(invert(blocks)):
            inverse[i, p, own, :] = entry
    for j in range(13):
        for e in range(3):
            for d in range(3):
                block = stencil[1 + j, e, d]
                coef[j * 9 + e * 3 + d, :, own, :] = block
                if j in ROLLED:
                    rolled[ROLLED.index(j) * 9 + e * 3 + d, :, own, :] = roll_z(
                        block, neighbour_steps[j][2]
                    )
    for c in range(K):
        for d in range(3):
            for p in range(2):
                i = (c * 3 + d) * 2 + p
                rim_dn[pl.ds(i, 1), :] = cands[c, d, p, 0:1]
                rim_up[pl.ds(i, 1), :] = cands[c, d, p, 7:8]
    for msg, ones, row in ((rim_dn, ONE_DN, 0), (rim_up, ONE_UP, 7)):
        for n, j in enumerate(ones):
            for e in range(3):
                for d in range(3):
                    for p in range(2):
                        at = RIM_S + n * 18 + (e * 3 + d) * 2 + p
                        msg[pl.ds(at, 1), :] = stencil[1 + j, e, d, p, row : row + 1]


def roll_z(x, by):
    return pltpu.roll(x, by % 128, x.ndim - 1)


HALO_A = [(j, n, 1) for j in STEP for n in range(9)]
HALO_B = (
    [(None, i, p) for i in range(6) for p in range(2)]
    + [(j, n, p) for j in FLAT for n in range(9) for p in range(2)]
    + [(j, n, 0) for j in STEP for n in range(9)]
)


def halo_shape(items):
    return struct(-(-4 * len(items) // 8) * 8, 128)


def pack_halo_kernel(items, stencil, inverse, halo_dn, halo_up):
    for k, (j, n, p) in enumerate(items):
        rows = pl.ds(4 * k, 4)
        if j is None:
            halo_dn[rows, :] = inverse[n, p, pl.ds(8, 4), :]
            halo_up[rows, :] = inverse[n, p, pl.ds(12, 4), :]
        else:
            halo_dn[rows, :] = stencil[1 + j, n // 3, n % 3, p, 0:4]
            halo_up[rows, :] = stencil[1 + j, n // 3, n % 3, p, 4:8]


def halo_rows(items, from_up, from_dn, coef, rolled, inverse):
    for msg, four in ((from_up, 16), (from_dn, 4)):
        for k, (j, n, p) in enumerate(items):
            block = msg[pl.ds(4 * k, 4), :]
            if j is None:
                inverse[n, p, pl.ds(four, 4), :] = block
                continue
            coef[j * 9 + n, p, pl.ds(four, 4), :] = block
            if j in ROLLED:
                at = ROLLED.index(j) * 9 + n
                rolled[at, p, pl.ds(four, 4), :] = roll_z(block, neighbour_steps[j][2])


def halo_a_kernel(from_up, from_dn, coef_in, rolled_in, coef, rolled):
    halo_rows(HALO_A, from_up, from_dn, coef, rolled, None)


def halo_b_kernel(from_up, from_dn, coef_in, rolled_in, inverse_in, _, coef, rolled, inverse):
    halo_rows(HALO_B, from_up, from_dn, coef, rolled, inverse)


def matrices(coef, rolled, far_coef=None, far_rolled=None):
    def get(j, e, d, plane, row, turned):
        n = (ROLLED.index(j) if turned else j) * 9 + e * 3 + d
        if plane >= 0:
            return (rolled if turned else coef)[n, plane, pl.ds(row, 8), :]
        n = (STEP_ROLLED.index(j) if turned else STEP.index(j)) * 9 + e * 3 + d
        return (far_rolled if turned else far_coef)[n, pl.ds(row, 8), :]

    return get


def gather_terms(matrix, load, base, half, terms):
    lane = lax.broadcasted_iota(jnp.int32, (8, 128), 1)
    acc = {}
    loads = {}

    def value(c, d, plane, oy):
        key = (c, d, plane, oy)
        if key not in loads:
            loads[key] = load((half * 4 + c) * 3 + d, plane, base + oy)
        return loads[key]

    def order(term):
        oy = neighbour_steps[term[2]][1]
        return term[1], -oy if term[3] else oy

    for cp, fp, j, transposed in sorted(terms, key=order):
        oy, oz = neighbour_steps[j][1:]
        for d in range(3):
            for e in range(3):
                if transposed:
                    m = matrix(j, d, e, cp, base - oy, False)
                    shift, row = -oz, -oy
                else:
                    m = matrix(j, e, d, cp, base, oz != 0)
                    shift, row = oz, oy
                for c in range(4):
                    t = m * value(c, d, fp, row)
                    key = (c, e, shift)
                    acc[key] = acc[key] + t if key in acc else t
    out = []
    for c in range(4):
        line = []
        for e in range(3):
            total = acc[c, e, 0]
            total = total + jnp.where(lane < 127, roll_z(acc[c, e, 1], -1), 0.0)
            total = total + jnp.where(lane > 0, roll_z(acc[c, e, -1], 1), 0.0)
            line.append(total)
        out.append(line)
    return out


TERMS = [
    [(0, 0, j, t) for j in FLAT for t in (False, True)] + [(0, 1, j, False) for j in STEP],
    [(1, 1, j, t) for j in FLAT for t in (False, True)] + [(0, 0, j, True) for j in STEP],
]
OUT_TERMS = [(1, 1, j, True) for j in STEP]
IN_TERMS = [(1, 2, j, False) for j in STEP]
LEFT_TERMS = [(-1, -1, j, True) for j in STEP]
FAR_TERMS = [(-1, 0, j, False) for j in STEP]


def from_frame(field):
    return lambda i, plane, row: field[i, plane, pl.ds(row, 8), :]


def tiles(bases, step, unrolled=2):
    if len(bases) == 1:
        for half in range(2):
            step(bases[0], half)
        return

    def one(i, carry):
        if unrolled == 2:
            step(bases[0] + i * 8, 0)
            step(bases[0] + i * 8, 1)
        else:
            step(bases[0] + (i // 2) * 8, i % 2)
        return carry

    lax.fori_loop(0, 2 * len(bases) // unrolled, one, 0)


def side_rows(lo, hi, items):
    return PAD + items * (hi - lo) + PAD


def spot(i, row, lo, hi):
    return PAD + i * (hi - lo) + row - lo


def outgoing(coef, field, msg, slot, bases, lo, hi):
    def step(base, half):
        got = gather_terms(matrices(coef, None), from_frame(field), base, half, OUT_TERMS)
        for c in range(4):
            for e in range(3):
                i = (half * 4 + c) * 3 + e
                msg[slot, pl.ds(spot(i, base, lo, hi), 8), :] = got[c][e]

    tiles(bases, step)


def plane_out(field, plane, msg, slot, lo, hi):
    for i in range(24):
        msg[slot, pl.ds(spot(i, lo, lo, hi), hi - lo), :] = field[i, plane, pl.ds(lo, hi - lo), :]


def send(coef, field, box, same, other, bases, lo, hi):
    right = parity()
    outgoing(coef, field, box, right, bases, lo, hi)
    plane_out(field, 0, box, 1 - right, lo, hi)
    same[...] = box[0]
    other[...] = box[1]


def first_kernel(from_up, from_dn, coef_in, field_in, coef, field, same, other, box):
    for msg, row, ones in ((from_up, 16, ONE_DN), (from_dn, 7, ONE_UP)):
        for i in range(24):
            for p in range(2):
                field[i, p, pl.ds(row, 1), :] = msg[pl.ds(2 * i + p, 1), :]
        for m, j in enumerate(ones):
            for n in range(9):
                for p in range(2):
                    at = RIM_S + m * 18 + n * 2 + p
                    coef[j * 9 + n, p, pl.ds(row, 1), :] = msg[pl.ds(at, 1), :]
    send(coef, field, box, same, other, *ROUNDS[0])


def second_kernel(from_up, from_dn, coef, field_in, field, same, other, box):
    for msg, row in ((from_up, 16), (from_dn, 4)):
        for i in range(24):
            for p in range(2):
                field[i, p, pl.ds(row, 4), :] = msg[pl.ds(4 * (2 * i + p), 4), :]
    send(coef, field, box, same, other, *ROUNDS[1])


SUMS = PAD + 24 * TALL
BOTH = SUMS + 24 * (TALL - 2) + PAD


def sum_spot(i, row):
    return SUMS + i * (TALL - 2) + row - LO - 1


def both_kernel(field, part, segs, same, other, box):
    right = parity()
    for plane, slot in ((1, right), (0, 1 - right)):
        for i in range(24):
            box[slot, pl.ds(spot(i, LO, LO, HI), TALL), :] = field[i, plane, pl.ds(LO, TALL), :]
            box[slot, pl.ds(sum_spot(i, LO + 1), TALL - 2), :] = part[i, plane, pl.ds(LO + 1, TALL - 2), :]
    box[right, pl.ds(0, 8), :] = segs[0]
    same[...] = box[0]
    other[...] = box[1]


def pack_far_kernel(coef, inverse, same, other, box):
    right = parity()
    for i in range(81):
        box[right, pl.ds(TALL * i, TALL), :] = coef[9 * STEP[0] + i, 1, pl.ds(LO, TALL), :]
    for i in range(6):
        box[right, pl.ds(TALL * (81 + i), TALL), :] = inverse[i, 1, pl.ds(LO, TALL), :]
        box[1 - right, pl.ds(TALL * (81 + i), TALL), :] = inverse[i, 0, pl.ds(LO, TALL), :]
    same[...] = box[0]
    other[...] = box[1]


def far_kernel(same, other, far_coef, far_rolled, far_inverse, box):
    box[0] = same[...]
    box[1] = other[...]
    right = parity()
    rows = pl.ds(LO, TALL)
    for k, j in enumerate(STEP):
        for n in range(9):
            block = box[1 - right, pl.ds(TALL * (9 * k + n), TALL), :]
            far_coef[9 * k + n, rows, :] = block
            if j in ROLLED:
                far_rolled[9 * STEP_ROLLED.index(j) + n, rows, :] = roll_z(block, neighbour_steps[j][2])
    for i in range(6):
        far_inverse[i, 0, rows, :] = box[1 - right, pl.ds(TALL * (81 + i), TALL), :]
        far_inverse[i, 1, rows, :] = box[right, pl.ds(TALL * (81 + i), TALL), :]


def beyond_kernel(bases, coef, far_coef, far_rolled, field, far_part):
    get = matrices(coef, None, far_coef, far_rolled)

    def step(base, half):
        for n, terms in enumerate((FAR_TERMS, OUT_TERMS)):
            got = gather_terms(get, from_frame(field), base, half, terms)
            for c in range(4):
                for e in range(3):
                    far_part[(half * 4 + c) * 3 + e, n, pl.ds(base, 8), :] = got[c][e]

    tiles(bases, step)


def relax(inverse, p, base, v, res):
    inv = [inverse[n, p, pl.ds(base, 8), :] * DAMPING for n in range(6)]
    out = []
    for e in range(3):
        move = inv[SYM_OF[e, 0]] * res[0] + inv[SYM_OF[e, 1]] * res[1] + inv[SYM_OF[e, 2]] * res[2]
        out.append((1.0 - DAMPING) * v[e] - move)
    return out


def four_kernel(bases, coef, rolled, far_coef, inverse, far_inverse, field, part, far_part, same, other, new, far, far_seg, box):
    box[0] = same[...]
    box[1] = other[...]
    right = parity()
    get = matrices(coef, rolled, far_coef)

    far_seg[0] = box[1 - right, pl.ds(0, 8), :]

    def message(side, at):
        return box[right if side else 1 - right, pl.ds(at, 8), :]

    def load(i, plane, row):
        return message(plane == 2, spot(i, row, LO, HI))

    def step(base, half):
        here = pl.ds(base, 8)
        for p, terms in enumerate((LEFT_TERMS, IN_TERMS)):
            got = gather_terms(get, load, base, half, terms)
            for c in range(4):
                at = (half * 4 + c) * 3
                res = [part[at + e, p, here, :] + got[c][e] for e in range(3)]
                out = relax(inverse, p, base, [field[at + e, p, here, :] for e in range(3)], res)
                for e in range(3):
                    new[at + e, p, here, :] = out[e]
                res = [message(p, sum_spot(at + e, base)) + far_part[at + e, p, here, :] for e in range(3)]
                out = relax(far_inverse, p, base, [load(at + e, 2 if p else -1, base) for e in range(3)], res)
                for e in range(3):
                    far[at + e, p, here, :] = out[e]

    tiles(bases, step)


def local_kernel(bases, coef, rolled, field, part):
    def step(base, half):
        for p in range(2):
            got = gather_terms(matrices(coef, rolled), from_frame(field), base, half, TERMS[p])
            for c in range(4):
                for e in range(3):
                    part[(half * 4 + c) * 3 + e, p, pl.ds(base, 8), :] = got[c][e]

    tiles(bases, step, 1)


def finish(coef, rolled, inverse, field, part, same, other, box, new, bases, lo, hi):
    box[0] = same[...]
    box[1] = other[...]
    right = parity()

    def load(i, plane, row):
        return box[right, pl.ds(spot(i, row, lo, hi), 8), :]

    def step(base, half):
        got = gather_terms(matrices(coef, rolled), load, base, half, IN_TERMS)
        for p in range(2):
            for c in range(4):
                at = (half * 4 + c) * 3
                res = []
                for e in range(3):
                    far = got[c][e] if p else box[1 - right, pl.ds(spot(at + e, base, lo, hi), 8), :]
                    res.append(part[at + e, p, pl.ds(base, 8), :] + far)
                out = relax(inverse, p, base, [field[at + e, p, pl.ds(base, 8), :] for e in range(3)], res)
                for e in range(3):
                    new[at + e, p, pl.ds(base, 8), :] = out[e]

    tiles(bases, step)


ROUNDS = [((8,), 7, 17), ((4, 12), 4, 20), ((4, 12), 5, 19)]
ALL = (4, 12)


def sweep_first(coef, rolled, inverse, field, part, same, other, seg, new, to_dn, to_up, box):
    finish(coef, rolled, inverse, field, part, same, other, box, new, *ROUNDS[0])
    for i in range(24):
        for p in range(2):
            to_dn[pl.ds(4 * (2 * i + p), 4), :] = new[i, p, pl.ds(8, 4), :]
            to_up[pl.ds(4 * (2 * i + p), 4), :] = new[i, p, pl.ds(12, 4), :]
    to_up[pl.ds(SEG_ROW, 1), :] = seg[0, 3:4].astype(F32)


def sweep_second(coef, rolled, inverse, field, part, same, other, new, same_out, other_out, box, box_out):
    finish(coef, rolled, inverse, field, part, same, other, box, new, *ROUNDS[1])
    send(coef, new, box_out, same_out, other_out, *ROUNDS[2])


def sweep_third(coef, rolled, inverse, field, part, same, other, new, box):
    finish(coef, rolled, inverse, field, part, same, other, box, new, *ROUNDS[2])


def segments_kernel(seg, from_dn, frame):
    frame[0] = jnp.zeros((8, 128), F32)
    frame[0, pl.ds(0, 1), :] = from_dn[pl.ds(SEG_ROW, 1), :]
    frame[0, pl.ds(1, 4), :] = seg[0].astype(F32)


def qr_kernel(field, far, seg, far_seg, prolongator, coarse):
    lane = lax.broadcasted_iota(jnp.int32, (8, 128), 1)
    valid_row = lax.broadcasted_iota(jnp.int32, (8, 128), 0) < 5
    numbers = [far_seg[0], seg[0]]
    joins = [
        [(by, (ids == roll_z(ids, -by)) & (lane + by >= 0) & (lane + by < 128)) for by in (-3, -2, -1, 1, 2, 3)]
        for ids in numbers
    ]

    def tree(op, parts):
        while len(parts) > 1:
            parts = [op(x, y) for x, y in zip(parts[::2], parts[1::2])] + parts[len(parts) // 2 * 2 :]
        return parts[0]

    def over_z(fx, op, x):
        return tree(op, [x] + [jnp.where(mask, roll_z(x, -by), 0.0) for by, mask in joins[fx]])

    def dot(fx, a, b):
        return over_z(fx, jnp.add, tree(jnp.add, [x * y for x, y in zip(a, b)]))

    def largest(fx, a):
        return over_z(fx, jnp.maximum, tree(jnp.maximum, [jnp.abs(x) for x in a]))

    ids = numbers[1]
    slot = lane.astype(F32)
    starts = jnp.zeros((8, 128), jnp.int32)
    for bit in (64, 32, 16, 8, 4, 2, 1):
        before = jnp.take_along_axis(ids, starts + (bit - 1), axis=1)
        starts = jnp.where(before < slot, starts + bit, starts)
    in_use = slot <= jnp.max(ids, axis=1, keepdims=True)

    def put(k, j, values):
        compact = jnp.take_along_axis(values, starts, axis=1)
        coarse[k, j, 0] = jnp.where(in_use, compact, 0.0)[1:5, 0:NSEG]

    cols = []
    for order in (((far, 0), (field, 0)), ((field, 1), (far, 1))):
        cols.append(
            [
                [
                    jnp.where(valid_row, ref[i * 3 + d, p, pl.ds(first, 8, stride=2), :], 1.0)
                    for ref, p in order
                    for first in (7, 8)
                    for d in range(3)
                ]
                for i in range(K)
            ]
        )
    tops = [largest(fx, cols[fx][0]) for fx in range(2)]
    for k in range(K):
        near = [[x * (0.125 / tops[fx]) for x in cols[fx][k]] for fx in range(2)]
        squares = [dot(fx, near[fx], near[fx]) for fx in range(2)]
        products = {(fx, j): dot(fx, near[fx], cols[fx][j]) for j in range(k + 1, K) for fx in range(2)}
        put(k, k, jnp.sqrt(squares[1]) * 8.0 * tops[1])
        if k < K - 1:
            tops = [largest(fx, cols[fx][k + 1]) for fx in range(2)]
        for fx in range(2):
            scale = lax.rsqrt(squares[fx])
            cols[fx][k] = [x * scale for x in near[fx]]
            for j in range(k + 1, K):
                r = products[fx, j] * scale
                cols[fx][j] = [x - r * y for x, y in zip(cols[fx][j], cols[fx][k])]
                if fx == 1:
                    put(k, j, r)
                    coarse[j, k, 0] = jnp.zeros((4, NSEG), F32)
        for fx in range(2):
            at = 6 * (1 - fx)
            for d in range(3):
                prolongator[k, d, fx, pl.ds(0, 4, stride=2), :] = cols[fx][k][at + 3 + d][0:4]
                prolongator[k, d, fx, pl.ds(1, 4, stride=2), :] = cols[fx][k][at + d][1:5]


def moved(block, axis, by):
    size = lax.axis_size(axis)
    return lax.ppermute(block, axis, [((i + by) % size, i) for i in range(size)])


def swapped(same, other):
    size = lax.axis_size("gx")
    pairs = [(i, i + 1) for i in range(0, size, 2)]
    around = [(i, (i + 1) % size) for i in range(1, size, 2)]
    return [
        lax.ppermute(block, "gx", two + [(j, i) for i, j in two])
        for block, two in ((same, pairs), (other, around))
    ]


def body(stencil, cands, seg):
    frame = struct(24, 2, ROWS, 128)
    operator = [struct(117, 2, ROWS, 128), struct(9 * len(ROLLED), 2, ROWS, 128), struct(6, 2, ROWS, 128)]
    rim_dn, rim_up, coef, rolled, inverse, field = call(
        pack_kernel, [struct(RIM, 128)] * 2 + operator + [frame], stencil, cands
    )
    rim_from_up = moved(rim_dn, "gy", 1)
    rim_from_dn = moved(rim_up, "gy", -1)

    edge = struct(EDGE, 128)
    sides = [struct(side_rows(lo, hi, 24), 128) for _, lo, hi in ROUNDS]
    boxes = [pltpu.VMEM((2, *side.shape), F32) for side in sides]

    def local(t):
        bases = ROUNDS[t][0] if t < 3 else ALL
        return call(functools.partial(local_kernel, bases), [frame], coef, rolled, field, us=1.7 if t else 0.9)[0]

    coef, field, same, other = call(
        first_kernel, [operator[0], frame, sides[0], sides[0]], rim_from_up, rim_from_dn, coef, field,
        aliases={2: 0, 3: 1}, scratch=boxes[:1],
    )
    same, other = swapped(same, other)
    halo = []
    for items in (HALO_A, HALO_B):
        halo_dn, halo_up = call(
            functools.partial(pack_halo_kernel, items), [halo_shape(items)] * 2, stencil, inverse, us=0.1
        )
        halo.append((moved(halo_dn, "gy", 1), moved(halo_up, "gy", -1)))
    part = local(0)
    field, to_dn, to_up = call(
        sweep_first, [frame, edge, edge], coef, rolled, inverse, field, part, same, other, seg, scratch=boxes[:1], us=4
    )
    from_up = moved(to_dn, "gy", 1)
    from_dn = moved(to_up, "gy", -1)
    segs = call(segments_kernel, [struct(1, 8, 128)], seg, from_dn)[0]
    coef, rolled = call(halo_a_kernel, operator[:2], *halo[0], coef, rolled, aliases={2: 0, 3: 1})
    field, same, other = call(
        second_kernel, [frame, sides[1], sides[1]], from_up, from_dn, coef, field,
        aliases={3: 0}, scratch=boxes[1:2], us=3,
    )
    coef, rolled, inverse = call(
        halo_b_kernel, operator, *halo[1], coef, rolled, inverse, field, aliases={2: 0, 3: 1, 4: 2}, after=1
    )
    same, other = swapped(same, other)
    part = local(1)
    across = struct(-(-TALL * 87 // 8) * 8, 128)
    across_box = pltpu.VMEM((2, *across.shape), F32)
    across_same, across_other = swapped(
        *call(pack_far_kernel, [across, across], coef, inverse, scratch=[across_box])
    )
    field, same, other = call(
        sweep_second, [frame, sides[2], sides[2]], coef, rolled, inverse, field, part, same, other, scratch=boxes[1:], us=1.3
    )
    same, other = swapped(same, other)
    part = local(2)
    far_coef, far_rolled, far_inverse = call(
        far_kernel,
        [struct(81, ROWS, 128), struct(9 * len(STEP_ROLLED), ROWS, 128), operator[2]],
        across_same, across_other, scratch=[across_box],
    )
    field = call(
        sweep_third, [frame], coef, rolled, inverse, field, part, same, other, scratch=boxes[2:], us=0.8
    )[0]
    part = local(3)
    side = struct(BOTH, 128)
    box = pltpu.VMEM((2, *side.shape), F32)
    same, other = swapped(
        *call(both_kernel, [side, side], field, part, segs, scratch=[box])
    )
    far_part = call(
        functools.partial(beyond_kernel, ALL), [frame], coef, far_coef, far_rolled, field, us=0.8
    )[0]
    field, far, far_seg = call(
        functools.partial(four_kernel, ALL), [frame, frame, struct(1, 8, 128)],
        coef, rolled, far_coef, inverse, far_inverse, field, part, far_part, same, other, scratch=[box],
    )
    prolongator, coarse = call(
        qr_kernel, [struct(K, 3, 2, 8, 128), struct(K, K, 1, 4, NSEG)], field, far, segs, far_seg, us=3.0
    )
    return prolongator, coarse


def solution(mesh):
    in_specs = (
        P(None, None, None, "gx", "gy", None),
        P(None, None, "gx", "gy", None),
        P("gx", "gy", None),
    )
    out_specs = (P(None, None, "gx", "gy", None), P(None, None, "gx", "gy", None))
    return jax.shard_map(body, mesh=mesh, in_specs=in_specs, out_specs=out_specs, check_vma=False)
```

```python
import functools

import jax
import jax.numpy as jnp
import numpy as np
from jax import lax
from jax.experimental import pallas as pl
from jax.experimental.pallas import tpu as pltpu
from jax.sharding import PartitionSpec as P

ITERS = 4
NSEG = 63
K = 8
DAMPING = 0.8
F32 = jnp.float32
neighbour_steps = [
    (sx, sy, sz)
    for sx in (-1, 0, 1)
    for sy in (-1, 0, 1)
    for sz in (-1, 0, 1)
    if (sx, sy, sz) > (0, 0, 0)
]
ROLLED = [j for j, o in enumerate(neighbour_steps) if o[2] != 0]
FLAT = [j for j, o in enumerate(neighbour_steps) if o[0] == 0]
STEP = [j for j, o in enumerate(neighbour_steps) if o[0] == 1]
STEP_ROLLED = [j for j in STEP if j in ROLLED]
SYM = [(0, 0), (0, 1), (0, 2), (1, 1), (1, 2), (2, 2)]
SYM_OF = {(e, d): SYM.index((min(e, d), max(e, d))) for e in range(3) for d in range(3)}
ROWS = 24
VMEM = pl.BlockSpec(memory_space=pltpu.VMEM)
ANY = pl.BlockSpec(memory_space=pl.ANY)
LIMIT = 12 * 2**20

ONE_DN = [j for j, o in enumerate(neighbour_steps) if o[1] == -1]
ONE_UP = [j for j, o in enumerate(neighbour_steps) if o[1] == 1]
RIM_S = 48
RIM = 160
SEG_ROW = 4 * 48
EDGE = SEG_ROW + 8
PAD = 8
LO, HI = 6, 18
TALL = HI - LO
FLOPS_PER_US = 1.1e9
BYTES_PER_US = 3.6e6


def call(kernel, out_shape, *args, us=0.3, aliases=None, scratch=(), after=0):
    return pl.pallas_call(
        kernel,
        out_shape=out_shape,
        in_specs=[VMEM] * (len(args) - after) + [ANY] * after,
        out_specs=jax.tree.map(lambda _: VMEM, out_shape),
        input_output_aliases=aliases or {},
        scratch_shapes=list(scratch),
        compiler_params=pltpu.CompilerParams(vmem_limit_bytes=LIMIT),
        cost_estimate=pl.CostEstimate(flops=int(us * FLOPS_PER_US), bytes_accessed=int(us * BYTES_PER_US), transcendentals=0),
    )(*args)


def parity():
    return lax.rem(lax.axis_index("gx"), 2)


def struct(*shape):
    return jax.ShapeDtypeStruct(shape, F32)


def invert(b):
    a00, a01, a02, a11, a12, a22 = b
    c00 = a11 * a22 - a12 * a12
    c01 = a12 * a02 - a01 * a22
    c02 = a01 * a12 - a11 * a02
    c11 = a00 * a22 - a02 * a02
    c12 = a01 * a02 - a00 * a12
    c22 = a00 * a11 - a01 * a01
    det = a00 * c00 + a01 * c01 + a02 * c02
    return [c / det for c in (c00, c01, c02, c11, c12, c22)]


def rim_kernel(stencil, cands, rim_dn, rim_up):
    for c in range(K):
        for d in range(3):
            for p in range(2):
                i = (c * 3 + d) * 2 + p
                rim_dn[pl.ds(i, 1), :] = cands[c, d, p, 0:1]
                rim_up[pl.ds(i, 1), :] = cands[c, d, p, 7:8]
    for msg, ones, row in ((rim_dn, ONE_DN, 0), (rim_up, ONE_UP, 7)):
        for n, j in enumerate(ones):
            for e in range(3):
                for d in range(3):
                    for p in range(2):
                        at = RIM_S + n * 18 + (e * 3 + d) * 2 + p
                        msg[pl.ds(at, 1), :] = stencil[1 + j, e, d, p, row : row + 1]


def own_kernel(stencil, cands, coef, rolled, inverse, field):
    own = pl.ds(8, 8)
    for c in range(K):
        for d in range(3):
            field[c * 3 + d, :, own, :] = cands[c, d]
    for p in range(2):
        blocks = [stencil[0, e, d, p] for e, d in SYM]
        for i, entry in enumerate(invert(blocks)):
            inverse[i, p, own, :] = entry
    for j in range(13):
        for e in range(3):
            for d in range(3):
                block = stencil[1 + j, e, d]
                coef[j * 9 + e * 3 + d, :, own, :] = block
                if j in ROLLED:
                    rolled[ROLLED.index(j) * 9 + e * 3 + d, :, own, :] = roll_z(
                        block, neighbour_steps[j][2]
                    )


def roll_z(x, by):
    return pltpu.roll(x, by % 128, x.ndim - 1)


HALO_A = [(j, n, 1) for j in STEP for n in range(9)]
HALO_B = (
    [(None, i, p) for i in range(6) for p in range(2)]
    + [(j, n, p) for j in FLAT for n in range(9) for p in range(2)]
    + [(j, n, 0) for j in STEP for n in range(9)]
)


def halo_shape(items):
    return struct(-(-4 * len(items) // 8) * 8, 128)


def pack_halo_kernel(items, stencil, inverse, halo_dn, halo_up):
    for k, (j, n, p) in enumerate(items):
        rows = pl.ds(4 * k, 4)
        if j is None:
            halo_dn[rows, :] = inverse[n, p, pl.ds(8, 4), :]
            halo_up[rows, :] = inverse[n, p, pl.ds(12, 4), :]
        else:
            halo_dn[rows, :] = stencil[1 + j, n // 3, n % 3, p, 0:4]
            halo_up[rows, :] = stencil[1 + j, n // 3, n % 3, p, 4:8]


def halo_rows(items, from_up, from_dn, coef, rolled, inverse):
    for msg, four in ((from_up, 16), (from_dn, 4)):
        for k, (j, n, p) in enumerate(items):
            block = msg[pl.ds(4 * k, 4), :]
            if j is None:
                inverse[n, p, pl.ds(four, 4), :] = block
                continue
            coef[j * 9 + n, p, pl.ds(four, 4), :] = block
            if j in ROLLED:
                at = ROLLED.index(j) * 9 + n
                rolled[at, p, pl.ds(four, 4), :] = roll_z(block, neighbour_steps[j][2])


def halo_a_kernel(from_up, from_dn, coef_in, rolled_in, coef, rolled):
    halo_rows(HALO_A, from_up, from_dn, coef, rolled, None)


def halo_b_kernel(from_up, from_dn, coef_in, rolled_in, inverse_in, _, coef, rolled, inverse):
    halo_rows(HALO_B, from_up, from_dn, coef, rolled, inverse)


def matrices(coef, rolled, far_coef=None, far_rolled=None):
    def get(j, e, d, plane, row, turned):
        n = (ROLLED.index(j) if turned else j) * 9 + e * 3 + d
        if plane >= 0:
            return (rolled if turned else coef)[n, plane, pl.ds(row, 8), :]
        n = (STEP_ROLLED.index(j) if turned else STEP.index(j)) * 9 + e * 3 + d
        return (far_rolled if turned else far_coef)[n, pl.ds(row, 8), :]

    return get


def gather_terms(matrix, load, base, half, terms):
    lane = lax.broadcasted_iota(jnp.int32, (8, 128), 1)
    acc = {}
    loads = {}

    def value(c, d, plane, oy):
        key = (c, d, plane, oy)
        if key not in loads:
            loads[key] = load((half * 4 + c) * 3 + d, plane, base + oy)
        return loads[key]

    def order(term):
        oy = neighbour_steps[term[2]][1]
        return term[1], -oy if term[3] else oy

    for cp, fp, j, transposed in sorted(terms, key=order):
        oy, oz = neighbour_steps[j][1:]
        for d in range(3):
            for e in range(3):
                if transposed:
                    m = matrix(j, d, e, cp, base - oy, False)
                    shift, row = -oz, -oy
                else:
                    m = matrix(j, e, d, cp, base, oz != 0)
                    shift, row = oz, oy
                for c in range(4):
                    t = m * value(c, d, fp, row)
                    key = (c, e, shift)
                    acc[key] = acc[key] + t if key in acc else t
    out = []
    for c in range(4):
        line = []
        for e in range(3):
            total = acc[c, e, 0]
            total = total + jnp.where(lane < 127, roll_z(acc[c, e, 1], -1), 0.0)
            total = total + jnp.where(lane > 0, roll_z(acc[c, e, -1], 1), 0.0)
            line.append(total)
        out.append(line)
    return out


TERMS = [
    [(0, 0, j, t) for j in FLAT for t in (False, True)] + [(0, 1, j, False) for j in STEP],
    [(1, 1, j, t) for j in FLAT for t in (False, True)] + [(0, 0, j, True) for j in STEP],
]
OUT_TERMS = [(1, 1, j, True) for j in STEP]
IN_TERMS = [(1, 2, j, False) for j in STEP]
LEFT_TERMS = [(-1, -1, j, True) for j in STEP]
FAR_TERMS = [(-1, 0, j, False) for j in STEP]


def from_frame(field):
    return lambda i, plane, row: field[i, plane, pl.ds(row, 8), :]


def tiles(bases, step, unrolled=2):
    if len(bases) == 1:
        for half in range(2):
            step(bases[0], half)
        return

    def one(i, carry):
        if unrolled == 2:
            step(bases[0] + i * 8, 0)
            step(bases[0] + i * 8, 1)
        else:
            step(bases[0] + (i // 2) * 8, i % 2)
        return carry

    lax.fori_loop(0, 2 * len(bases) // unrolled, one, 0)


def side_rows(lo, hi, items):
    return PAD + items * (hi - lo) + PAD


def spot(i, row, lo, hi):
    return PAD + i * (hi - lo) + row - lo


def outgoing(coef, field, msg, slot, bases, lo, hi):
    def step(base, half):
        got = gather_terms(matrices(coef, None), from_frame(field), base, half, OUT_TERMS)
        for c in range(4):
            for e in range(3):
                i = (half * 4 + c) * 3 + e
                msg[slot, pl.ds(spot(i, base, lo, hi), 8), :] = got[c][e]

    tiles(bases, step)


def plane_out(field, plane, msg, slot, lo, hi):
    for i in range(24):
        msg[slot, pl.ds(spot(i, lo, lo, hi), hi - lo), :] = field[i, plane, pl.ds(lo, hi - lo), :]


def send(coef, field, box, same, other, bases, lo, hi):
    right = parity()
    outgoing(coef, field, box, right, bases, lo, hi)
    plane_out(field, 0, box, 1 - right, lo, hi)
    same[...] = box[0]
    other[...] = box[1]


def first_kernel(from_up, from_dn, coef_in, field_in, coef, field, same, other, box):
    for msg, row, ones in ((from_up, 16, ONE_DN), (from_dn, 7, ONE_UP)):
        for i in range(24):
            for p in range(2):
                field[i, p, pl.ds(row, 1), :] = msg[pl.ds(2 * i + p, 1), :]
        for m, j in enumerate(ones):
            for n in range(9):
                for p in range(2):
                    at = RIM_S + m * 18 + n * 2 + p
                    coef[j * 9 + n, p, pl.ds(row, 1), :] = msg[pl.ds(at, 1), :]
    send(coef, field, box, same, other, *ROUNDS[0])


def second_kernel(from_up, from_dn, coef, field_in, field, same, other, box):
    for msg, row in ((from_up, 16), (from_dn, 4)):
        for i in range(24):
            for p in range(2):
                field[i, p, pl.ds(row, 4), :] = msg[pl.ds(4 * (2 * i + p), 4), :]
    send(coef, field, box, same, other, *ROUNDS[1])


SUMS = PAD + 24 * TALL
BOTH = SUMS + 24 * (TALL - 2) + PAD


def sum_spot(i, row):
    return SUMS + i * (TALL - 2) + row - LO - 1


def both_kernel(field, part, segs, same, other, box):
    right = parity()
    for plane, slot in ((1, right), (0, 1 - right)):
        for i in range(24):
            box[slot, pl.ds(spot(i, LO, LO, HI), TALL), :] = field[i, plane, pl.ds(LO, TALL), :]
            box[slot, pl.ds(sum_spot(i, LO + 1), TALL - 2), :] = part[i, plane, pl.ds(LO + 1, TALL - 2), :]
    box[right, pl.ds(0, 8), :] = segs[0]
    same[...] = box[0]
    other[...] = box[1]


def pack_far_kernel(coef, inverse, same, other, box):
    right = parity()
    for i in range(81):
        box[right, pl.ds(TALL * i, TALL), :] = coef[9 * STEP[0] + i, 1, pl.ds(LO, TALL), :]
    for i in range(6):
        box[right, pl.ds(TALL * (81 + i), TALL), :] = inverse[i, 1, pl.ds(LO, TALL), :]
        box[1 - right, pl.ds(TALL * (81 + i), TALL), :] = inverse[i, 0, pl.ds(LO, TALL), :]
    same[...] = box[0]
    other[...] = box[1]


def far_kernel(same, other, far_coef, far_rolled, far_inverse, box):
    box[0] = same[...]
    box[1] = other[...]
    right = parity()
    rows = pl.ds(LO, TALL)
    for k, j in enumerate(STEP):
        for n in range(9):
            block = box[1 - right, pl.ds(TALL * (9 * k + n), TALL), :]
            far_coef[9 * k + n, rows, :] = block
            if j in ROLLED:
                far_rolled[9 * STEP_ROLLED.index(j) + n, rows, :] = roll_z(block, neighbour_steps[j][2])
    for i in range(6):
        far_inverse[i, 0, rows, :] = box[1 - right, pl.ds(TALL * (81 + i), TALL), :]
        far_inverse[i, 1, rows, :] = box[right, pl.ds(TALL * (81 + i), TALL), :]


def beyond_kernel(bases, coef, far_coef, far_rolled, field, far_part):
    get = matrices(coef, None, far_coef, far_rolled)

    def step(base, half):
        for n, terms in enumerate((FAR_TERMS, OUT_TERMS)):
            got = gather_terms(get, from_frame(field), base, half, terms)
            for c in range(4):
                for e in range(3):
                    far_part[(half * 4 + c) * 3 + e, n, pl.ds(base, 8), :] = got[c][e]

    tiles(bases, step)


def relax(inverse, p, base, v, res):
    inv = [inverse[n, p, pl.ds(base, 8), :] * DAMPING for n in range(6)]
    out = []
    for e in range(3):
        move = inv[SYM_OF[e, 0]] * res[0] + inv[SYM_OF[e, 1]] * res[1] + inv[SYM_OF[e, 2]] * res[2]
        out.append((1.0 - DAMPING) * v[e] - move)
    return out


def four_kernel(bases, coef, rolled, far_coef, inverse, far_inverse, field, part, far_part, same, other, new, far, far_seg, box):
    box[0] = same[...]
    box[1] = other[...]
    right = parity()
    get = matrices(coef, rolled, far_coef)

    far_seg[0] = box[1 - right, pl.ds(0, 8), :]

    def message(side, at):
        return box[right if side else 1 - right, pl.ds(at, 8), :]

    def load(i, plane, row):
        return message(plane == 2, spot(i, row, LO, HI))

    def step(base, half):
        here = pl.ds(base, 8)
        for p, terms in enumerate((LEFT_TERMS, IN_TERMS)):
            got = gather_terms(get, load, base, half, terms)
            for c in range(4):
                at = (half * 4 + c) * 3
                res = [part[at + e, p, here, :] + got[c][e] for e in range(3)]
                out = relax(inverse, p, base, [field[at + e, p, here, :] for e in range(3)], res)
                for e in range(3):
                    new[at + e, p, here, :] = out[e]
                res = [message(p, sum_spot(at + e, base)) + far_part[at + e, p, here, :] for e in range(3)]
                out = relax(far_inverse, p, base, [load(at + e, 2 if p else -1, base) for e in range(3)], res)
                for e in range(3):
                    far[at + e, p, here, :] = out[e]

    tiles(bases, step)


def local_kernel(bases, coef, rolled, field, part):
    def step(base, half):
        for p in range(2):
            got = gather_terms(matrices(coef, rolled), from_frame(field), base, half, TERMS[p])
            for c in range(4):
                for e in range(3):
                    part[(half * 4 + c) * 3 + e, p, pl.ds(base, 8), :] = got[c][e]

    tiles(bases, step, 1)


def finish(coef, rolled, inverse, field, part, same, other, box, new, bases, lo, hi):
    box[0] = same[...]
    box[1] = other[...]
    right = parity()

    def load(i, plane, row):
        return box[right, pl.ds(spot(i, row, lo, hi), 8), :]

    def step(base, half):
        got = gather_terms(matrices(coef, rolled), load, base, half, IN_TERMS)
        for p in range(2):
            for c in range(4):
                at = (half * 4 + c) * 3
                res = []
                for e in range(3):
                    far = got[c][e] if p else box[1 - right, pl.ds(spot(at + e, base, lo, hi), 8), :]
                    res.append(part[at + e, p, pl.ds(base, 8), :] + far)
                out = relax(inverse, p, base, [field[at + e, p, pl.ds(base, 8), :] for e in range(3)], res)
                for e in range(3):
                    new[at + e, p, pl.ds(base, 8), :] = out[e]

    tiles(bases, step)


ROUNDS = [((8,), 7, 17), ((4, 12), 4, 20), ((4, 12), 5, 19)]
ALL = (4, 12)


def sweep_first(coef, rolled, inverse, field, part, same, other, seg, new, to_dn, to_up, box):
    finish(coef, rolled, inverse, field, part, same, other, box, new, *ROUNDS[0])
    for i in range(24):
        for p in range(2):
            to_dn[pl.ds(4 * (2 * i + p), 4), :] = new[i, p, pl.ds(8, 4), :]
            to_up[pl.ds(4 * (2 * i + p), 4), :] = new[i, p, pl.ds(12, 4), :]
    to_up[pl.ds(SEG_ROW, 1), :] = seg[0, 3:4].astype(F32)


def sweep_second(coef, rolled, inverse, field, part, same, other, new, same_out, other_out, box, box_out):
    finish(coef, rolled, inverse, field, part, same, other, box, new, *ROUNDS[1])
    send(coef, new, box_out, same_out, other_out, *ROUNDS[2])


def sweep_third(coef, rolled, inverse, field, part, same, other, new, box):
    finish(coef, rolled, inverse, field, part, same, other, box, new, *ROUNDS[2])


def segments_kernel(seg, from_dn, frame):
    frame[0] = jnp.zeros((8, 128), F32)
    frame[0, pl.ds(0, 1), :] = from_dn[pl.ds(SEG_ROW, 1), :]
    frame[0, pl.ds(1, 4), :] = seg[0].astype(F32)


def qr_kernel(field, far, seg, far_seg, prolongator, coarse):
    lane = lax.broadcasted_iota(jnp.int32, (8, 128), 1)
    valid_row = lax.broadcasted_iota(jnp.int32, (8, 128), 0) < 5
    numbers = [far_seg[0], seg[0]]
    joins = [
        [(by, (ids == roll_z(ids, -by)) & (lane + by >= 0) & (lane + by < 128)) for by in (-3, -2, -1, 1, 2, 3)]
        for ids in numbers
    ]

    def tree(op, parts):
        while len(parts) > 1:
            parts = [op(x, y) for x, y in zip(parts[::2], parts[1::2])] + parts[len(parts) // 2 * 2 :]
        return parts[0]

    def over_z(fx, op, x):
        return tree(op, [x] + [jnp.where(mask, roll_z(x, -by), 0.0) for by, mask in joins[fx]])

    def dot(fx, a, b):
        return over_z(fx, jnp.add, tree(jnp.add, [x * y for x, y in zip(a, b)]))

    def largest(fx, a):
        return over_z(fx, jnp.maximum, tree(jnp.maximum, [jnp.abs(x) for x in a]))

    ids = numbers[1]
    slot = lane.astype(F32)
    starts = jnp.zeros((8, 128), jnp.int32)
    for bit in (64, 32, 16, 8, 4, 2, 1):
        before = jnp.take_along_axis(ids, starts + (bit - 1), axis=1)
        starts = jnp.where(before < slot, starts + bit, starts)
    in_use = slot <= jnp.max(ids, axis=1, keepdims=True)

    def put(k, j, values):
        compact = jnp.take_along_axis(values, starts, axis=1)
        coarse[k, j, 0] = jnp.where(in_use, compact, 0.0)[1:5, 0:NSEG]

    cols = []
    for order in (((far, 0), (field, 0)), ((field, 1), (far, 1))):
        cols.append(
            [
                [
                    jnp.where(valid_row, ref[i * 3 + d, p, pl.ds(first, 8, stride=2), :], 1.0)
                    for ref, p in order
                    for first in (7, 8)
                    for d in range(3)
                ]
                for i in range(K)
            ]
        )
    tops = [largest(fx, cols[fx][0]) for fx in range(2)]
    for k in range(K):
        near = [[x * (0.125 / tops[fx]) for x in cols[fx][k]] for fx in range(2)]
        squares = [dot(fx, near[fx], near[fx]) for fx in range(2)]
        products = {(fx, j): dot(fx, near[fx], cols[fx][j]) for j in range(k + 1, K) for fx in range(2)}
        put(k, k, jnp.sqrt(squares[1]) * 8.0 * tops[1])
        if k < K - 1:
            tops = [largest(fx, cols[fx][k + 1]) for fx in range(2)]
        for fx in range(2):
            scale = lax.rsqrt(squares[fx])
            cols[fx][k] = [x * scale for x in near[fx]]
            for j in range(k + 1, K):
                r = products[fx, j] * scale
                cols[fx][j] = [x - r * y for x, y in zip(cols[fx][j], cols[fx][k])]
                if fx == 1:
                    put(k, j, r)
                    coarse[j, k, 0] = jnp.zeros((4, NSEG), F32)
        for fx in range(2):
            at = 6 * (1 - fx)
            for d in range(3):
                prolongator[k, d, fx, pl.ds(0, 4, stride=2), :] = cols[fx][k][at + 3 + d][0:4]
                prolongator[k, d, fx, pl.ds(1, 4, stride=2), :] = cols[fx][k][at + d][1:5]


def moved(block, axis, by):
    size = lax.axis_size(axis)
    return lax.ppermute(block, axis, [((i + by) % size, i) for i in range(size)])


def swapped(same, other):
    size = lax.axis_size("gx")
    pairs = [(i, i + 1) for i in range(0, size, 2)]
    around = [(i, (i + 1) % size) for i in range(1, size, 2)]
    return [
        lax.ppermute(block, "gx", two + [(j, i) for i, j in two])
        for block, two in ((same, pairs), (other, around))
    ]


def body(stencil, cands, seg):
    frame = struct(24, 2, ROWS, 128)
    operator = [struct(117, 2, ROWS, 128), struct(9 * len(ROLLED), 2, ROWS, 128), struct(6, 2, ROWS, 128)]
    rim_dn, rim_up = call(rim_kernel, [struct(RIM, 128)] * 2, stencil, cands)
    coef, rolled, inverse, field = call(own_kernel, operator + [frame], stencil, cands)
    rim_from_up = moved(rim_dn, "gy", 1)
    rim_from_dn = moved(rim_up, "gy", -1)

    edge = struct(EDGE, 128)
    sides = [struct(side_rows(lo, hi, 24), 128) for _, lo, hi in ROUNDS]
    boxes = [pltpu.VMEM((2, *side.shape), F32) for side in sides]

    def local(t):
        bases = ROUNDS[t][0] if t < 3 else ALL
        return call(functools.partial(local_kernel, bases), [frame], coef, rolled, field, us=1.7 if t else 0.9)[0]

    coef, field, same, other = call(
        first_kernel, [operator[0], frame, sides[0], sides[0]], rim_from_up, rim_from_dn, coef, field,
        aliases={2: 0, 3: 1}, scratch=boxes[:1],
    )
    same, other = swapped(same, other)
    halo = []
    for items in (HALO_A, HALO_B):
        halo_dn, halo_up = call(
            functools.partial(pack_halo_kernel, items), [halo_shape(items)] * 2, stencil, inverse, us=0.1
        )
        halo.append((moved(halo_dn, "gy", 1), moved(halo_up, "gy", -1)))
    part = local(0)
    field, to_dn, to_up = call(
        sweep_first, [frame, edge, edge], coef, rolled, inverse, field, part, same, other, seg, scratch=boxes[:1], us=4
    )
    from_up = moved(to_dn, "gy", 1)
    from_dn = moved(to_up, "gy", -1)
    segs = call(segments_kernel, [struct(1, 8, 128)], seg, from_dn)[0]
    coef, rolled = call(halo_a_kernel, operator[:2], *halo[0], coef, rolled, aliases={2: 0, 3: 1})
    field, same, other = call(
        second_kernel, [frame, sides[1], sides[1]], from_up, from_dn, coef, field,
        aliases={3: 0}, scratch=boxes[1:2], us=3,
    )
    coef, rolled, inverse = call(
        halo_b_kernel, operator, *halo[1], coef, rolled, inverse, field, aliases={2: 0, 3: 1, 4: 2}, after=1
    )
    same, other = swapped(same, other)
    part = local(1)
    across = struct(-(-TALL * 87 // 8) * 8, 128)
    across_box = pltpu.VMEM((2, *across.shape), F32)
    across_same, across_other = swapped(
        *call(pack_far_kernel, [across, across], coef, inverse, scratch=[across_box])
    )
    field, same, other = call(
        sweep_second, [frame, sides[2], sides[2]], coef, rolled, inverse, field, part, same, other, scratch=boxes[1:], us=1.3
    )
    same, other = swapped(same, other)
    part = local(2)
    far_coef, far_rolled, far_inverse = call(
        far_kernel,
        [struct(81, ROWS, 128), struct(9 * len(STEP_ROLLED), ROWS, 128), operator[2]],
        across_same, across_other, scratch=[across_box],
    )
    field = call(
        sweep_third, [frame], coef, rolled, inverse, field, part, same, other, scratch=boxes[2:], us=0.8
    )[0]
    part = local(3)
    side = struct(BOTH, 128)
    box = pltpu.VMEM((2, *side.shape), F32)
    same, other = swapped(
        *call(both_kernel, [side, side], field, part, segs, scratch=[box])
    )
    far_part = call(
        functools.partial(beyond_kernel, ALL), [frame], coef, far_coef, far_rolled, field, us=0.8
    )[0]
    field, far, far_seg = call(
        functools.partial(four_kernel, ALL), [frame, frame, struct(1, 8, 128)],
        coef, rolled, far_coef, inverse, far_inverse, field, part, far_part, same, other, scratch=[box],
    )
    prolongator, coarse = call(
        qr_kernel, [struct(K, 3, 2, 8, 128), struct(K, K, 1, 4, NSEG)], field, far, segs, far_seg, us=3.0
    )
    return prolongator, coarse


def solution(mesh):
    in_specs = (
        P(None, None, None, "gx", "gy", None),
        P(None, None, "gx", "gy", None),
        P("gx", "gy", None),
    )
    out_specs = (P(None, None, "gx", "gy", None), P(None, None, "gx", "gy", None))
    return jax.shard_map(body, mesh=mesh, in_specs=in_specs, out_specs=out_specs, check_vma=False)
```
